128 devices in a mesh: blk: 8 (over z, x_lo), dp: 16 (over x_hi, y, core).
Axes of the slice: x: 4 (x_hi: 2, x_lo: 2; x = x_hi * 2 + x_lo), y: 4, z: 4, core: 2. Of those that a mesh axis runs over, the one named last changes fastest.
Arguments:
- queries: bfloat16 [16, 8192, 2560], P('dp', 'blk'), may hold values from -16 to 16, as said below
- candidates: bfloat16 [16, 1024, 2560], P('dp', 'blk'), may hold values from -6 to 6, as said below
- loss_weight: float32 [16, 8192], P('dp', 'blk'), may hold values from 8 to 80
- positives: int32 [16, 8192], P('dp', 'blk'), may hold values from 0 to 1023
- producers: int32 [16, 1024, 1], P('dp', 'blk'), may hold values from 0 to 127; in each aligned block of 128 rows (0 to 127, 128 to 255, ..., all dimensions but the last counted through in order) at most 4 rows name the same one
- rows: int32 [16, 1024], P('dp', 'blk'), may hold values from 0 to 255
Outputs:
- query_grad: bfloat16 [16, 8192, 2560], P('dp', 'blk')
- decoder_grad: float32 [32768, 2560], P(('blk', 'dp'))
The draws below stay inside these ranges and needn't reach their ends.
Inputs may be any that keep to these rules, and one draw needn't show every extreme that they name: `producers`: decoder shard s is the device with blk index s // (number of dp devices) and dp index s % (number of dp devices). Among the 128 hypotheses on one device no decoder shard appears more than 4 times, and in every draw some device has a shard that appears exactly 4 times. `queries`: Real-valued embeddings. `candidates`: Real-valued embeddings.
All inputs are finite; a program needn't handle non-finite values.
Results may differ from the reference program's by a relative error of at most 0.005.
Values may be sent and summed in bfloat16 or wider, within the bound.
A program may use at most 128 MiB of HBM per device.

```python
import math
import jax
import jax.numpy as jnp
import numpy as np
from jax import lax

D = 2560
CB = 128
HR = 256
MOST = 4
NQG = 8192
NCG = 1024
SHARDS = 128
N_DP = 16


def draw_candidates(key, part):
    key = jax.random.fold_in(key, 11)
    return jax.random.truncated_normal(key, -6.0, 6.0, (N_DP, NCG, D), jnp.float32).astype(jnp.bfloat16)


def draw_queries(key, part):
    key = jax.random.fold_in(key, 12)
    return jax.random.truncated_normal(key, -6.0, 6.0, (N_DP, NQG, D), jnp.float32).astype(jnp.bfloat16)


def set_ends(values, rng, least, top_value):
    longest = values.shape.index(max(values.shape))
    spots = []
    for shift in (0, 1):
        where = [jax.random.randint(jax.random.fold_in(rng, axis), (), 0, length) for axis, length in enumerate(values.shape)]
        where[longest] = (where[longest] + shift) % values.shape[longest]
        spots.append(tuple(where))
    return values.at[spots[0]].set(least).at[spots[1]].set(top_value)


def levels(key, shape, pieces, least, largest):
    def one(axis_at, parts):
        heights = jax.random.uniform(jax.random.fold_in(jax.random.fold_in(key, 6), axis_at), (parts,), jnp.float32, least / len(pieces), largest / len(pieces))
        return jnp.repeat(jnp.exp(heights), shape[axis_at] // parts).reshape((-1,) + (1,) * (len(shape) - axis_at - 1))

    factor_of = one(*pieces[0])
    for cut in pieces[1:]:
        factor_of = factor_of * one(*cut)
    return factor_of


def shared_out(own_key, own, number, rows, number_of, top, reach, skew):
    sequence = jax.random.permutation(own_key, number_of)
    crowded, common = portions_of(number_of, rows * top, reach, skew, True), portions_of(number_of, rows * top, reach, skew, False)
    places = jnp.arange(number_of)

    def named(tallies, offset_by):
        used = int((tallies > 0).sum())
        fixed = max(1, used // 4)
        passed = fixed + (places - fixed + offset_by * (used - fixed)) % max(1, number_of - fixed)
        return jnp.zeros((number_of,), jnp.int32).at[sequence[jnp.where(places < fixed, places, passed)]].set(jnp.asarray(tallies, jnp.int32))

    tallies = jnp.where(number % 4 == 0, named(crowded, number // 4), named(common, number - number // 4 - 1))
    mixed = jax.random.permutation(jax.random.fold_in(own, 3), number_of)
    source_of, receiver = mixed[0:number_of // 2 * 2:2], mixed[1:number_of // 2 * 2:2]
    room = jnp.minimum(tallies[source_of] - 1, reach - tallies[receiver]) // 2
    room = jnp.where((source_of == sequence[0]) | (receiver == sequence[0]) | (tallies[receiver] == 0), 0, jnp.maximum(room, 0))
    passed = jax.random.randint(jax.random.fold_in(own, 4), (number_of // 2,), 0, 1 << 20) % (room + 1)
    tallies = tallies.at[source_of].add(-passed).at[receiver].add(passed)
    labels = jnp.searchsorted(jnp.cumsum(tallies), jnp.arange(rows * top), side="right").astype(jnp.int32)
    grid = labels.reshape(top, rows).T
    grid = grid[jax.random.permutation(jax.random.fold_in(own, 1), rows)]
    offset_by = jax.random.randint(jax.random.fold_in(own, 2), (rows, 1), 0, top)
    return jnp.take_along_axis(grid, (jnp.arange(top)[None, :] + offset_by) % top, axis=1)


def portions_of(number_of, total, most, slope, full):
    portions = [(1 << 20) // math.isqrt(grade ** slope) + 1 for grade in range(1, number_of + 1)]
    largest = most if full else min(most, max(-(-total // number_of), total * portions[0] // sum(portions)))
    least = 1 if total - largest >= number_of - 1 else 0
    holding, rest = [largest] + [least] * (number_of - 1), total - largest - least * (number_of - 1)
    while rest > 0:
        free = [i for i in range(1, number_of) if holding[i] < largest] or [i for i in range(1, number_of) if holding[i] < most]
        whole, left = sum([portions[i] for i in free]), rest
        for i in free:
            more = min(most - holding[i], max(1, left * portions[i] // whole), rest)
            holding[i] = holding[i] + more
            rest = rest - more
    return np.array(holding)


def setup_inputs(seed: int = 0) -> dict:
    arg_keys = jax.random.split(jax.random.key(seed), 7)
    queries = draw_queries(jax.random.fold_in(arg_keys[6], 71), 0)
    candidates = draw_candidates(jax.random.fold_in(arg_keys[6], 71), 0)
    loss_weight = jnp.clip(jnp.exp(math.log(80.0) - 2.3025851 * jax.random.uniform(arg_keys[2], (N_DP, NQG), jnp.float32) ** levels(arg_keys[2], (N_DP, NQG), ((0, 16), (1, 8)), -0.2, 0.2)), 8.0, 80.0)
    positives = set_ends(jax.random.randint(arg_keys[3], (N_DP, NQG), 0, NCG), jax.random.fold_in(arg_keys[3], 1), 0, NCG - 1).astype(jnp.int32)
    producers_keys = jax.random.split(jax.random.fold_in(arg_keys[4], 1), N_DP * NCG // CB)
    producers_turns = jax.random.permutation(jax.random.fold_in(arg_keys[4], 3), N_DP * NCG // CB)
    producers = jax.vmap(lambda own, number: shared_out(jax.random.fold_in(arg_keys[4], 2), own, number, CB, SHARDS, 1, MOST, 2))(producers_keys, producers_turns).reshape((N_DP, NCG, 1))
    rows = set_ends(jax.random.randint(arg_keys[5], (N_DP, NCG), 0, HR), jax.random.fold_in(arg_keys[5], 1), 0, HR - 1).astype(jnp.int32)
    return {"queries": queries, "candidates": candidates, "loss_weight": loss_weight, "positives": positives, "producers": producers, "rows": rows}


def group_gradients(query_rows, cand_rows, weight, target):
    scale_factor = 1.0 / math.sqrt(D)
    scores = jnp.dot(query_rows, cand_rows.T, preferred_element_type=jnp.float32) * scale_factor
    row_max = lax.optimization_barrier(jnp.max(scores, axis=1, keepdims=True))
    shifted = jnp.exp(scores - row_max)
    chance = shifted / lax.optimization_barrier(jnp.sum(shifted, axis=1, keepdims=True))
    column_ids = jnp.arange(NCG, dtype=jnp.int32)
    onehot = (column_ids[None, :] == target[:, None]).astype(jnp.float32)
    coefficient = (weight[:, None] * (chance - onehot)).astype(jnp.bfloat16)
    query_grad = (jnp.dot(coefficient, cand_rows, preferred_element_type=jnp.float32) * scale_factor).astype(jnp.bfloat16)
    cand_grad = jnp.dot(coefficient.T, query_rows, preferred_element_type=jnp.float32) * scale_factor
    return (query_grad, cand_grad)

def reference(queries, candidates, loss_weight, positives, producers, rows):
    query_grad, cand_grad = lax.map(lambda packed: group_gradients(*packed), (queries, candidates, loss_weight, positives))
    segment_ids = (producers[:, :, 0] * HR + rows).astype(jnp.int32).reshape(-1)
    decoder_grad = jax.ops.segment_sum(cand_grad.reshape(-1, D), segment_ids, num_segments=SHARDS * HR)
    return (query_grad, decoder_grad)
```

```python
import functools
import math

import jax
import jax.numpy as jnp
from jax import lax
from jax.experimental import pallas as pl
from jax.experimental.pallas import tpu as pltpu
from jax.sharding import PartitionSpec as P

D = 2560
HR = 256
MOST = 4
NQ = 1024
CB = 128
HB = 64
NC = 5
CW = D // NC
SHARDS = 128
SCALE = 1.0 / math.sqrt(D)
F32, BF16, I32 = jnp.float32, jnp.bfloat16, jnp.int32

SELF, XN, ZP, ZM, Z2 = 0, 2, 4, 6, 8
ZPX, ZMX, Z2X = (10, 13), (11, 14), (12, 15)
GROUPS = ((0, 4), (4, 4), (8, 5), (13, 3))

MESSAGES = (
    (0, 2, "x"), (2, 2, "p"), (4, 2, "m"), (6, 1, "p"), (7, 1, "m"),
    (8, 1, "p"), (9, 1, "m"), (10, 2, "x"), (12, 1, "p"), (13, 1, "m"),
)
NM = len(MESSAGES)


def main_kernel(
    q_hbm, c_hbm, w_ref, pos_ref, trow_ref, tcol_ref, qg_hbm, slots_ref,
    q, c, e, coef_t, coef, prod, snd, rcv, qg, sel, gs, mx, sm,
    q_sem, c_sem, ag_send, ag_recv, rs_send, rs_recv, qg_sem,
):
    blk = lax.axis_index("blk")
    z, x = blk // 2, blk % 2

    def at(dz, dx):
        return ((z + dz) % 4) * 2 + (x + dx) % 2

    peers = {"x": at(0, 1), "p": at(1, 0), "m": at(3, 0)}

    q_copy = pltpu.make_async_copy(q_hbm.at[0], q, q_sem)
    q_copy.start()
    own = [
        pltpu.make_async_copy(c_hbm.at[0, pl.ds(h * HB, HB)], c.at[h], c_sem.at[h]) for h in (0, 1)
    ]
    for copy in own:
        copy.start()

    barrier = pltpu.get_barrier_semaphore()
    for peer in peers.values():
        pl.semaphore_signal(
            barrier, inc=1, device_id={"blk": peer}, device_id_type=pl.DeviceIdType.MESH
        )
    pl.semaphore_wait(barrier, 3)

    def ag(src, dst, way):
        source = c_hbm.at[0, pl.ds(src * HB, HB)] if src < 2 else c.at[src]
        return pltpu.make_async_remote_copy(
            src_ref=source,
            dst_ref=c.at[dst],
            send_sem=ag_send.at[dst],
            recv_sem=ag_recv.at[dst],
            device_id={"blk": peers[way]},
            device_id_type=pl.DeviceIdType.MESH,
        )

    gather = {
        ZM: ag(0, ZM, "p"), ZP + 1: ag(1, ZP + 1, "m"), XN: ag(0, XN, "x"),
        ZM + 1: ag(1, ZM + 1, "p"), ZP: ag(0, ZP, "m"), XN + 1: ag(1, XN + 1, "x"),
        Z2: ag(ZM, Z2, "p"), Z2 + 1: ag(ZP + 1, Z2 + 1, "m"),
        ZMX[0]: ag(XN, ZMX[0], "p"), ZPX[0]: ag(XN, ZPX[0], "m"),
        ZMX[1]: ag(XN + 1, ZMX[1], "p"), ZPX[1]: ag(XN + 1, ZPX[1], "m"),
        Z2X[0]: ag(Z2, Z2X[0], "x"), Z2X[1]: ag(Z2 + 1, Z2X[1], "x"),
    }
    for slot in (ZM, ZP + 1, XN, ZM + 1, ZP, XN + 1):
        gather[slot].start()

    earlier = (tcol_ref[...] == trow_ref[...]) & (
        lax.broadcasted_iota(I32, (CB, CB), 0) < lax.broadcasted_iota(I32, (CB, CB), 1)
    )
    place = jnp.sum(earlier.astype(I32), axis=0, keepdims=True)
    slot_index = trow_ref[...] * MOST + place
    keys = jnp.concatenate([slot_index * 4 + part for part in range(4)], axis=1)

    def fill(i, _):
        row = i * 256 + lax.broadcasted_iota(I32, (256, 4 * CB), 0)
        key = ((row // 16) * MOST + row % 4) * 4 + (row // 4) % 4
        sel[pl.ds(pl.multiple_of(i * 256, 256), 256), :] = (key == keys).astype(F32).astype(BF16)
        return 0

    lax.fori_loop(0, 16 * SHARDS // 256, fill, 0)
    q_copy.wait()
    for copy in own:
        copy.wait()

    def scores(which):
        first, number = GROUPS[which]

        def part(i, _):
            span = pl.ds(pl.multiple_of(i * 256, 256), 256)
            s = lax.dot_general(
                c[first : first + number].reshape(number * HB, D), q[span, :],
                (((1,), (1,)), ((), ())), preferred_element_type=F32,
            ) * SCALE
            top = jnp.max(s, axis=0, keepdims=True)
            shifted = jnp.exp(s - top)
            e[first : first + number, :, span] = shifted.reshape(number, HB, 256)
            mx[which : which + 1, span] = top
            sm[which : which + 1, span] = jnp.sum(shifted, axis=0, keepdims=True)
            return 0

        lax.fori_loop(0, NQ // 256, part, 0)

    gather[ZM].wait_recv()
    gather[Z2].start()
    gather[ZP + 1].wait_recv()
    gather[Z2 + 1].start()
    gather[XN].wait_recv()
    gather[XN + 1].wait_recv()
    scores(0)
    gather[ZM + 1].wait_recv()
    gather[ZP].wait_recv()
    scores(1)
    gather[Z2].wait_recv()
    gather[Z2X[0]].start()
    gather[Z2 + 1].wait_recv()
    gather[Z2X[1]].start()
    for slot in (ZMX[0], ZPX[0], ZMX[1], ZPX[1]):
        gather[slot].start()
    for slot in (ZPX[0], ZMX[0], Z2X[0]):
        gather[slot].wait_recv()
    scores(2)
    for slot in (ZPX[1], ZMX[1], Z2X[1]):
        gather[slot].wait_recv()
    scores(3)

    top = jnp.max(mx[0:4], axis=0, keepdims=True)
    rescale = jnp.exp(mx[0:4] - top)
    inverse = 1.0 / jnp.sum(rescale * sm[0:4], axis=0, keepdims=True)
    weight, target = w_ref[...], pos_ref[...]
    places = {
        0: at(0, 0), 2: at(0, 1), 4: at(1, 0), 6: at(3, 0), 8: at(2, 0),
    }
    starts = [0] * 16
    for first, owner in places.items():
        starts[first], starts[first + 1] = owner * CB, owner * CB + HB
    for (low, high), owner in ((ZPX, at(1, 1)), (ZMX, at(3, 1)), (Z2X, at(2, 1))):
        starts[low], starts[high] = owner * CB, owner * CB + HB
    for which, (first, number) in enumerate(GROUPS):
        factor = rescale[which : which + 1] * inverse
        for k in range(first, first + number):
            ids = starts[k] + lax.broadcasted_iota(I32, (HB, NQ), 0)
            onehot = (ids == target).astype(F32)
            coef_t[k] = (weight * (e[k] * factor - onehot)).astype(BF16)

    def message(m, chunk):
        first, number, way = MESSAGES[m]
        return pltpu.make_async_remote_copy(
            src_ref=snd.at[chunk, pl.ds(first, number)],
            dst_ref=rcv.at[chunk, pl.ds(first, number)],
            send_sem=rs_send.at[chunk, m],
            recv_sem=rs_recv.at[chunk, m],
            device_id={"blk": peers[way]},
            device_id_type=pl.DeviceIdType.MESH,
        )

    def qg_copy(chunk):
        return pltpu.make_async_copy(
            qg.at[chunk],
            qg_hbm.at[0, :, pl.ds(pl.multiple_of(chunk * CW, CW), CW)],
            qg_sem.at[chunk],
        )

    def put(chunk, slot, value):
        snd[chunk, slot] = value.astype(BF16)

    def got(chunk, slot):
        return rcv[chunk, slot].astype(F32)

    def step(i, _):
        @pl.when(i < NC)
        def _():
            for half in range(CW // 256):
                columns = pl.ds(pl.multiple_of(i * CW + half * 256, 256), 256)
                block = jnp.dot(
                    coef_t[...].reshape(16 * HB, NQ), q[:, columns], preferred_element_type=F32
                ) * SCALE
                prod[i, :, :, half * 256 : half * 256 + 256] = block.reshape(16, HB, 256)
            put(i, 0, prod[i, Z2X[0]])
            put(i, 1, prod[i, Z2X[1]])
            message(0, i).start()
            put(i, 2, prod[i, ZPX[0]])
            put(i, 3, prod[i, ZPX[1]])
            message(1, i).start()
            put(i, 4, prod[i, ZMX[0]])
            put(i, 5, prod[i, ZMX[1]])
            message(2, i).start()
            put(i, 6, prod[i, ZP])
            message(3, i).start()
            put(i, 7, prod[i, ZM + 1])
            message(4, i).start()

        @pl.when(i == 0)
        def _():
            for k in range(4):
                coef[pl.ds(k * 256, 256), :] = jnp.transpose(
                    coef_t[:, :, k * 256 : k * 256 + 256].reshape(16 * HB, 256)
                )

        @pl.when(i < NC)
        def _():
            for half in range(CW // 256):
                columns = pl.ds(pl.multiple_of(i * CW + half * 256, 256), 256)
                total = jnp.dot(
                    coef[...], c[:, :, columns].reshape(16 * HB, 256), preferred_element_type=F32
                )
                qg[i, :, half * 256 : half * 256 + 256] = (total * SCALE).astype(BF16)
            qg_copy(i).start()

        @pl.when((i >= 1) & (i <= NC))
        def _():
            k = i - 1
            message(0, k).wait_recv()
            put(k, 9, prod[k, Z2] + got(k, 0))
            message(6, k).start()
            put(k, 8, prod[k, Z2 + 1] + got(k, 1))
            message(5, k).start()
            message(1, k).wait_recv()
            message(2, k).wait_recv()
            put(k, 10, prod[k, XN] + got(k, 2) + got(k, 4))
            put(k, 11, prod[k, XN + 1] + got(k, 3) + got(k, 5))
            message(7, k).start()

        @pl.when((i >= 2) & (i <= NC + 1))
        def _():
            k = i - 2
            message(5, k).wait_recv()
            put(k, 12, prod[k, ZP + 1] + got(k, 8))
            message(8, k).start()
            message(6, k).wait_recv()
            put(k, 13, prod[k, ZM] + got(k, 9))
            message(9, k).start()

        @pl.when(i >= 3)
        def _():
            k = i - 3
            for m in (3, 4, 7, 8, 9):
                message(m, k).wait_recv()
            low = prod[k, SELF] + got(k, 6) + got(k, 13) + got(k, 10)
            high = prod[k, SELF + 1] + got(k, 7) + got(k, 12) + got(k, 11)
            for part in range(4):
                gs[part * CB : part * CB + HB, :] = low[:, part * 128 : part * 128 + 128].astype(BF16)
                gs[part * CB + HB : part * CB + CB, :] = high[
                    :, part * 128 : part * 128 + 128
                ].astype(BF16)
            picked = jnp.dot(sel[...], gs[...], preferred_element_type=F32)
            slots_ref[:, :, pl.ds(pl.multiple_of(k * 128, 128), 128)] = picked.astype(BF16).reshape(
                SHARDS, 16, 128
            )

        return 0

    lax.fori_loop(0, NC + 3, step, 0)

    for copy in gather.values():
        copy.wait_send()

    def drain(i, _):
        for m in range(NM):
            message(m, i).wait_send()
        qg_copy(i).wait()
        return 0

    lax.fori_loop(0, NC, drain, 0)


def key_kernel(me_ref, shard_ref, row_ref, key_ref):
    hits = (shard_ref[...] == me_ref[0]).astype(F32)
    before = (
        lax.broadcasted_iota(I32, (CB, CB), 0) < lax.broadcasted_iota(I32, (CB, CB), 1)
    ).astype(F32)
    place = jnp.dot(hits.astype(BF16), before.astype(BF16), preferred_element_type=F32)
    numbers = (row_ref[...] + 1).astype(F32) * hits
    lanes = lax.broadcasted_iota(I32, (SHARDS, 16 * SHARDS), 1)
    spread = (lanes // 16 == lax.broadcasted_iota(I32, (SHARDS, 16 * SHARDS), 0)).astype(F32)
    spread = spread.astype(BF16)
    slot = lax.broadcasted_iota(I32, (8, 16 * SHARDS), 1) % 4
    total = jnp.zeros((8, 16 * SHARDS), F32)
    for k in range(MOST):
        chosen = jnp.where(place == float(k), numbers, 0.0).astype(BF16)
        by_source = lax.dot_general(
            jnp.ones((8, CB), BF16), chosen, (((1,), (1,)), ((), ())), preferred_element_type=F32
        )
        wide = jnp.dot(by_source.astype(BF16), spread, preferred_element_type=F32)
        total = total + jnp.where(slot == k, wide, 0.0)
    key_ref[...] = total.astype(I32) - 1


def landing_kernel(key_ref, arrived_ref, out_ref, land):
    key = key_ref[0:1, :]
    part = (lax.broadcasted_iota(I32, (1, 16 * SHARDS), 1) // 4) % 4
    rows = lax.broadcasted_iota(I32, (HR, 16 * SHARDS), 0)
    for k in range(4):
        land[k * HR : k * HR + HR, :] = (rows == jnp.where(part == k, key, -1)).astype(F32).astype(BF16)
    for chunk in range(NC):
        total = jnp.dot(
            land[...],
            arrived_ref[:, :, chunk * 128 : chunk * 128 + 128].reshape(16 * SHARDS, 128),
            preferred_element_type=F32,
        )
        for k in range(4):
            first = chunk * CW + k * 128
            out_ref[:, first : first + 128] = total[k * HR : k * HR + HR]


def per_device(queries, candidates, loss_weight, positives, producers, rows):
    vmem, hbm = pl.BlockSpec(memory_space=pltpu.VMEM), pl.BlockSpec(memory_space=pl.ANY)
    shard_row = producers.reshape(1, CB)
    shard_column = producers.reshape(CB, 1)
    meta = lax.all_gather(
        jnp.concatenate([shard_row, rows], axis=0), ("blk", "dp"), axis=0, tiled=False
    )
    query_grad, slots = pl.pallas_call(
        main_kernel,
        out_shape=(
            jax.ShapeDtypeStruct((1, NQ, D), BF16),
            jax.ShapeDtypeStruct((SHARDS, 16, D // 4), BF16),
        ),
        in_specs=[hbm, hbm, vmem, vmem, vmem, vmem],
        out_specs=(hbm, vmem),
        scratch_shapes=[
            pltpu.VMEM((NQ, D), BF16),
            pltpu.VMEM((16, HB, D), BF16),
            pltpu.VMEM((16, HB, NQ), F32),
            pltpu.VMEM((16, HB, NQ), BF16),
            pltpu.VMEM((NQ, 16 * HB), BF16),
            pltpu.VMEM((NC, 16, HB, CW), F32),
            pltpu.VMEM((NC, 14, HB, CW), BF16),
            pltpu.VMEM((NC, 14, HB, CW), BF16),
            pltpu.VMEM((NC, NQ, CW), BF16),
            pltpu.VMEM((16 * SHARDS, 4 * CB), BF16),
            pltpu.VMEM((4 * CB, 128), BF16),
            pltpu.VMEM((8, NQ), F32),
            pltpu.VMEM((8, NQ), F32),
            pltpu.SemaphoreType.DMA,
            pltpu.SemaphoreType.DMA((2,)),
            pltpu.SemaphoreType.DMA((16,)),
            pltpu.SemaphoreType.DMA((16,)),
            pltpu.SemaphoreType.DMA((NC, NM)),
            pltpu.SemaphoreType.DMA((NC, NM)),
            pltpu.SemaphoreType.DMA((NC,)),
        ],
        compiler_params=pltpu.CompilerParams(
            collective_id=0, has_side_effects=True, vmem_limit_bytes=60 * 2**20
        ),
        cost_estimate=pl.CostEstimate(
            flops=6 * NQ * NQ * D, bytes_accessed=14 * 2**20, transcendentals=NQ * NQ
        ),
        name="gather_scores_reduce",
    )(queries, candidates, loss_weight, positives, shard_row, shard_column)
    arrived = lax.all_to_all(slots, ("blk", "dp"), split_axis=0, concat_axis=0, tiled=True)
    me = lax.axis_index("blk") * lax.axis_size("dp") + lax.axis_index("dp")
    key = pl.pallas_call(
        key_kernel,
        out_shape=jax.ShapeDtypeStruct((8, 16 * SHARDS), I32),
        in_specs=[pl.BlockSpec(memory_space=pltpu.SMEM), vmem, vmem],
        out_specs=vmem,
        name="slot_rows",
    )(me.astype(I32).reshape(1), meta[:, 0], meta[:, 1])
    decoder_grad = pl.pallas_call(
        landing_kernel,
        out_shape=jax.ShapeDtypeStruct((HR, D), F32),
        in_specs=[vmem, vmem],
        out_specs=vmem,
        scratch_shapes=[pltpu.VMEM((4 * HR, 16 * SHARDS), BF16)],
        compiler_params=pltpu.CompilerParams(vmem_limit_bytes=40 * 2**20),
        name="landing",
    )(key, arrived)
    return query_grad, decoder_grad


def solution(mesh):
    return jax.shard_map(
        per_device,
        mesh=mesh,
        in_specs=(
            P("dp", "blk", None),
            P("dp", "blk", None),
            P("dp", "blk"),
            P("dp", "blk"),
            P("dp", "blk", None),
            P("dp", "blk"),
        ),
        out_specs=(P("dp", "blk", None), P(("blk", "dp"), None)),
        check_vma=False,
    )
```

```python
import functools
import math

import jax
import jax.numpy as jnp
from jax import lax
from jax.experimental import pallas as pl
from jax.experimental.pallas import tpu as pltpu
from jax.sharding import PartitionSpec as P

D = 2560
HR = 256
MOST = 4
NQ = 1024
CB = 128
HB = 64
NC = 5
CW = D // NC
SHARDS = 128
SCALE = 1.0 / math.sqrt(D)
F32, BF16, I32 = jnp.float32, jnp.bfloat16, jnp.int32

SELF, XN, ZP, ZM, Z2 = 0, 2, 4, 6, 8
ZPX, ZMX, Z2X = (10, 13), (11, 14), (12, 15)
GROUPS = ((0, 4), (4, 4), (8, 5), (13, 3))

MESSAGES = (
    (0, 2, "x"), (2, 2, "p"), (4, 2, "m"), (6, 1, "p"), (7, 1, "m"),
    (8, 1, "p"), (9, 1, "m"), (10, 2, "x"), (12, 1, "p"), (13, 1, "m"),
)
NM = len(MESSAGES)


def main_kernel(
    q_hbm, c_hbm, w_ref, pos_ref, shard_ref, row_ref, qg_hbm, slots_ref, key_ref,
    q, c, e, coef_t, coef, prod, snd, rcv, qg, sel, gs, mx, sm, told, heard,
    q_sem, c_sem, ag_send, ag_recv, rs_send, rs_recv, qg_sem, tell_sem, hear_sem, self_sem,
):
    blk, dp = lax.axis_index("blk"), lax.axis_index("dp")
    n_dp = lax.axis_size("dp")
    me = blk * n_dp + dp
    z, x = blk // 2, blk % 2

    def at(dz, dx):
        return ((z + dz) % 4) * 2 + (x + dx) % 2

    peers = {"x": at(0, 1), "p": at(1, 0), "m": at(3, 0)}

    q_copy = pltpu.make_async_copy(q_hbm.at[0], q, q_sem)
    q_copy.start()
    own = [
        pltpu.make_async_copy(c_hbm.at[0, pl.ds(h * HB, HB)], c.at[h], c_sem.at[h]) for h in (0, 1)
    ]
    for copy in own:
        copy.start()

    barrier = pltpu.get_barrier_semaphore()

    def other(i):
        peer = (me + i) % SHARDS
        return peer, {"blk": peer // n_dp, "dp": peer % n_dp}

    def greet(i, _):
        pl.semaphore_signal(
            barrier, inc=1, device_id=other(i)[1], device_id_type=pl.DeviceIdType.MESH
        )
        return 0

    lax.fori_loop(1, SHARDS, greet, 0)
    pl.semaphore_wait(barrier, SHARDS - 1)

    def ag(src, dst, way):
        source = c_hbm.at[0, pl.ds(src * HB, HB)] if src < 2 else c.at[src]
        return pltpu.make_async_remote_copy(
            src_ref=source,
            dst_ref=c.at[dst],
            send_sem=ag_send.at[dst],
            recv_sem=ag_recv.at[dst],
            device_id={"blk": peers[way]},
            device_id_type=pl.DeviceIdType.MESH,
        )

    gather = {
        ZM: ag(0, ZM, "p"), ZP + 1: ag(1, ZP + 1, "m"), XN: ag(0, XN, "x"),
        ZM + 1: ag(1, ZM + 1, "p"), ZP: ag(0, ZP, "m"), XN + 1: ag(1, XN + 1, "x"),
        Z2: ag(ZM, Z2, "p"), Z2 + 1: ag(ZP + 1, Z2 + 1, "m"),
        ZMX[0]: ag(XN, ZMX[0], "p"), ZPX[0]: ag(XN, ZPX[0], "m"),
        ZMX[1]: ag(XN + 1, ZMX[1], "p"), ZPX[1]: ag(XN + 1, ZPX[1], "m"),
        Z2X[0]: ag(Z2, Z2X[0], "x"), Z2X[1]: ag(Z2 + 1, Z2X[1], "x"),
    }
    for slot in (ZM, ZP + 1, XN, ZM + 1, ZP, XN + 1):
        gather[slot].start()

    shard = shard_ref[...]
    wide = jnp.broadcast_to(shard, (CB, CB))
    earlier = (jnp.transpose(wide) == wide) & (
        lax.broadcasted_iota(I32, (CB, CB), 0) < lax.broadcasted_iota(I32, (CB, CB), 1)
    )
    place = jnp.sum(earlier.astype(I32), axis=0, keepdims=True)
    slot_index = shard * MOST + place
    keys = jnp.concatenate([slot_index * 4 + part for part in range(4)], axis=1)

    hit = (lax.broadcasted_iota(I32, (8 * SHARDS, CB), 0) // 8 == shard).astype(F32).astype(BF16)
    number = jnp.where(
        lax.broadcasted_iota(I32, (128, CB), 0) == place, row_ref[...] + 1, 0
    ).astype(F32).astype(BF16)
    told[...] = lax.dot_general(
        hit, number, (((1,), (1,)), ((), ())), preferred_element_type=F32
    ).astype(I32).reshape(SHARDS, 8, 128)

    def tell(i, _):
        peer, device = other(i)
        pltpu.make_async_remote_copy(
            src_ref=told.at[peer], dst_ref=heard.at[me], send_sem=tell_sem, recv_sem=hear_sem,
            device_id=device, device_id_type=pl.DeviceIdType.MESH,
        ).start()
        return 0

    lax.fori_loop(1, SHARDS, tell, 0)
    note = pltpu.make_async_copy(told.at[me], heard.at[me], self_sem)
    note.start()

    def fill(i, _):
        row = i * 256 + lax.broadcasted_iota(I32, (256, 4 * CB), 0)
        key = ((row // 16) * MOST + row % 4) * 4 + (row // 4) % 4
        sel[pl.ds(pl.multiple_of(i * 256, 256), 256), :] = (key == keys).astype(F32).astype(BF16)
        return 0

    lax.fori_loop(0, 16 * SHARDS // 256, fill, 0)
    q_copy.wait()
    for copy in own:
        copy.wait()

    def scores(which):
        first, number = GROUPS[which]

        def part(i, _):
            span = pl.ds(pl.multiple_of(i * 256, 256), 256)
            s = lax.dot_general(
                c[first : first + number].reshape(number * HB, D), q[span, :],
                (((1,), (1,)), ((), ())), preferred_element_type=F32,
            ) * SCALE
            top = jnp.max(s, axis=0, keepdims=True)
            shifted = jnp.exp(s - top)
            e[first : first + number, :, span] = shifted.reshape(number, HB, 256)
            mx[which : which + 1, span] = top
            sm[which : which + 1, span] = jnp.sum(shifted, axis=0, keepdims=True)
            return 0

        lax.fori_loop(0, NQ // 256, part, 0)

    gather[ZM].wait_recv()
    gather[Z2].start()
    gather[ZP + 1].wait_recv()
    gather[Z2 + 1].start()
    gather[XN].wait_recv()
    gather[XN + 1].wait_recv()
    scores(0)
    gather[ZM + 1].wait_recv()
    gather[ZP].wait_recv()
    scores(1)
    gather[Z2].wait_recv()
    gather[Z2X[0]].start()
    gather[Z2 + 1].wait_recv()
    gather[Z2X[1]].start()
    for slot in (ZMX[0], ZPX[0], ZMX[1], ZPX[1]):
        gather[slot].start()
    for slot in (ZPX[0], ZMX[0], Z2X[0]):
        gather[slot].wait_recv()
    scores(2)
    for slot in (ZPX[1], ZMX[1], Z2X[1]):
        gather[slot].wait_recv()
    scores(3)

    top = jnp.max(mx[0:4], axis=0, keepdims=True)
    rescale = jnp.exp(mx[0:4] - top)
    inverse = 1.0 / jnp.sum(rescale * sm[0:4], axis=0, keepdims=True)
    weight, target = w_ref[...], pos_ref[...]
    places = {
        0: at(0, 0), 2: at(0, 1), 4: at(1, 0), 6: at(3, 0), 8: at(2, 0),
    }
    starts = [0] * 16
    for first, owner in places.items():
        starts[first], starts[first + 1] = owner * CB, owner * CB + HB
    for (low, high), owner in ((ZPX, at(1, 1)), (ZMX, at(3, 1)), (Z2X, at(2, 1))):
        starts[low], starts[high] = owner * CB, owner * CB + HB
    for which, (first, number) in enumerate(GROUPS):
        factor = rescale[which : which + 1] * inverse
        for k in range(first, first + number):
            ids = starts[k] + lax.broadcasted_iota(I32, (HB, NQ), 0)
            onehot = (ids == target).astype(F32)
            coef_t[k] = (weight * (e[k] * factor - onehot)).astype(BF16)

    def message(m, chunk):
        first, number, way = MESSAGES[m]
        return pltpu.make_async_remote_copy(
            src_ref=snd.at[chunk, pl.ds(first, number)],
            dst_ref=rcv.at[chunk, pl.ds(first, number)],
            send_sem=rs_send.at[chunk, m],
            recv_sem=rs_recv.at[chunk, m],
            device_id={"blk": peers[way]},
            device_id_type=pl.DeviceIdType.MESH,
        )

    def qg_copy(chunk):
        return pltpu.make_async_copy(
            qg.at[chunk],
            qg_hbm.at[0, :, pl.ds(pl.multiple_of(chunk * CW, CW), CW)],
            qg_sem.at[chunk],
        )

    def put(chunk, slot, value):
        snd[chunk, slot] = value.astype(BF16)

    def got(chunk, slot):
        return rcv[chunk, slot].astype(F32)

    def step(i, _):
        @pl.when(i < NC)
        def _():
            for half in range(CW // 256):
                columns = pl.ds(pl.multiple_of(i * CW + half * 256, 256), 256)
                block = jnp.dot(
                    coef_t[...].reshape(16 * HB, NQ), q[:, columns], preferred_element_type=F32
                ) * SCALE
                prod[i, :, :, half * 256 : half * 256 + 256] = block.reshape(16, HB, 256)
            put(i, 0, prod[i, Z2X[0]])
            put(i, 1, prod[i, Z2X[1]])
            message(0, i).start()
            put(i, 2, prod[i, ZPX[0]])
            put(i, 3, prod[i, ZPX[1]])
            message(1, i).start()
            put(i, 4, prod[i, ZMX[0]])
            put(i, 5, prod[i, ZMX[1]])
            message(2, i).start()
            put(i, 6, prod[i, ZP])
            message(3, i).start()
            put(i, 7, prod[i, ZM + 1])
            message(4, i).start()

        @pl.when(i == 0)
        def _():
            for k in range(4):
                coef[pl.ds(k * 256, 256), :] = jnp.transpose(
                    coef_t[:, :, k * 256 : k * 256 + 256].reshape(16 * HB, 256)
                )

        @pl.when(i < NC)
        def _():
            for half in range(CW // 256):
                columns = pl.ds(pl.multiple_of(i * CW + half * 256, 256), 256)
                total = jnp.dot(
                    coef[...], c[:, :, columns].reshape(16 * HB, 256), preferred_element_type=F32
                )
                qg[i, :, half * 256 : half * 256 + 256] = (total * SCALE).astype(BF16)
            qg_copy(i).start()

        @pl.when((i >= 1) & (i <= NC))
        def _():
            k = i - 1
            message(0, k).wait_recv()
            put(k, 9, prod[k, Z2] + got(k, 0))
            message(6, k).start()
            put(k, 8, prod[k, Z2 + 1] + got(k, 1))
            message(5, k).start()
            message(1, k).wait_recv()
            message(2, k).wait_recv()
            put(k, 10, prod[k, XN] + got(k, 2) + got(k, 4))
            put(k, 11, prod[k, XN + 1] + got(k, 3) + got(k, 5))
            message(7, k).start()

        @pl.when(i == 2)
        def _():
            pltpu.make_async_copy(
                heard.at[pl.ds(0, SHARDS - 1)], heard.at[pl.ds(0, SHARDS - 1)], hear_sem
            ).wait()
            note.wait()
            lanes = lax.broadcasted_iota(I32, (SHARDS, 16 * SHARDS), 1)
            spread = lanes // 16 == lax.broadcasted_iota(I32, (SHARDS, 16 * SHARDS), 0)
            unit = lax.broadcasted_iota(I32, (8, 128), 0) == lax.broadcasted_iota(I32, (8, 128), 1)
            by_slot = lax.dot_general(
                unit.astype(F32).astype(BF16), heard[:, 0, :].astype(F32).astype(BF16),
                (((1,), (1,)), ((), ())), preferred_element_type=F32,
            )
            wide = jnp.dot(
                by_slot.astype(BF16), spread.astype(F32).astype(BF16), preferred_element_type=F32
            )
            slot = lax.broadcasted_iota(I32, (8, 16 * SHARDS), 1) % 4
            mine = lax.broadcasted_iota(I32, (8, 16 * SHARDS), 0) == slot
            key = jnp.sum(jnp.where(mine, wide, 0.0), axis=0, keepdims=True).astype(I32) - 1
            key_ref[...] = jnp.broadcast_to(key, (8, 16 * SHARDS))

        @pl.when((i >= 2) & (i <= NC + 1))
        def _():
            k = i - 2
            message(5, k).wait_recv()
            put(k, 12, prod[k, ZP + 1] + got(k, 8))
            message(8, k).start()
            message(6, k).wait_recv()
            put(k, 13, prod[k, ZM] + got(k, 9))
            message(9, k).start()

        @pl.when(i >= 3)
        def _():
            k = i - 3
            for m in (3, 4, 7, 8, 9):
                message(m, k).wait_recv()
            low = prod[k, SELF] + got(k, 6) + got(k, 13) + got(k, 10)
            high = prod[k, SELF + 1] + got(k, 7) + got(k, 12) + got(k, 11)
            for part in range(4):
                gs[part * CB : part * CB + HB, :] = low[:, part * 128 : part * 128 + 128].astype(BF16)
                gs[part * CB + HB : part * CB + CB, :] = high[
                    :, part * 128 : part * 128 + 128
                ].astype(BF16)
            picked = jnp.dot(sel[...], gs[...], preferred_element_type=F32)
            slots_ref[:, :, pl.ds(pl.multiple_of(k * 128, 128), 128)] = picked.astype(BF16).reshape(
                SHARDS, 16, 128
            )

        return 0

    lax.fori_loop(0, NC + 3, step, 0)

    for copy in gather.values():
        copy.wait_send()

    def drain(i, _):
        for m in range(NM):
            message(m, i).wait_send()
        qg_copy(i).wait()
        return 0

    lax.fori_loop(0, NC, drain, 0)
    pltpu.make_async_copy(
        told.at[pl.ds(0, SHARDS - 1)], told.at[pl.ds(0, SHARDS - 1)], tell_sem
    ).wait()


def landing_kernel(key_ref, arrived_ref, out_ref, land):
    key = key_ref[0:1, :]
    part = (lax.broadcasted_iota(I32, (1, 16 * SHARDS), 1) // 4) % 4
    rows = lax.broadcasted_iota(I32, (HR, 16 * SHARDS), 0)
    for k in range(4):
        land[k * HR : k * HR + HR, :] = (rows == jnp.where(part == k, key, -1)).astype(F32).astype(BF16)
    for chunk in range(NC):
        total = jnp.dot(
            land[...],
            arrived_ref[:, :, chunk * 128 : chunk * 128 + 128].reshape(16 * SHARDS, 128),
            preferred_element_type=F32,
        )
        for k in range(4):
            first = chunk * CW + k * 128
            out_ref[:, first : first + 128] = total[k * HR : k * HR + HR]


def per_device(queries, candidates, loss_weight, positives, producers, rows):
    vmem, hbm = pl.BlockSpec(memory_space=pltpu.VMEM), pl.BlockSpec(memory_space=pl.ANY)
    shard_row = producers.reshape(1, CB)
    query_grad, slots, key = pl.pallas_call(
        main_kernel,
        out_shape=(
            jax.ShapeDtypeStruct((1, NQ, D), BF16),
            jax.ShapeDtypeStruct((SHARDS, 16, D // 4), BF16),
            jax.ShapeDtypeStruct((8, 16 * SHARDS), I32),
        ),
        in_specs=[hbm, hbm, vmem, vmem, vmem, vmem],
        out_specs=(hbm, vmem, vmem),
        scratch_shapes=[
            pltpu.VMEM((NQ, D), BF16),
            pltpu.VMEM((16, HB, D), BF16),
            pltpu.VMEM((16, HB, NQ), F32),
            pltpu.VMEM((16, HB, NQ), BF16),
            pltpu.VMEM((NQ, 16 * HB), BF16),
            pltpu.VMEM((NC, 16, HB, CW), F32),
            pltpu.VMEM((NC, 14, HB, CW), BF16),
            pltpu.VMEM((NC, 14, HB, CW), BF16),
            pltpu.VMEM((NC, NQ, CW), BF16),
            pltpu.VMEM((16 * SHARDS, 4 * CB), BF16),
            pltpu.VMEM((4 * CB, 128), BF16),
            pltpu.VMEM((8, NQ), F32),
            pltpu.VMEM((8, NQ), F32),
            pltpu.VMEM((SHARDS, 8, 128), I32),
            pltpu.VMEM((SHARDS, 8, 128), I32),
            pltpu.SemaphoreType.DMA,
            pltpu.SemaphoreType.DMA((2,)),
            pltpu.SemaphoreType.DMA((16,)),
            pltpu.SemaphoreType.DMA((16,)),
            pltpu.SemaphoreType.DMA((NC, NM)),
            pltpu.SemaphoreType.DMA((NC, NM)),
            pltpu.SemaphoreType.DMA((NC,)),
            pltpu.SemaphoreType.DMA,
            pltpu.SemaphoreType.DMA,
            pltpu.SemaphoreType.DMA,
        ],
        compiler_params=pltpu.CompilerParams(
            collective_id=0, has_side_effects=True, vmem_limit_bytes=60 * 2**20
        ),
        cost_estimate=pl.CostEstimate(
            flops=6 * NQ * NQ * D, bytes_accessed=14 * 2**20, transcendentals=NQ * NQ
        ),
        name="gather_scores_reduce",
    )(queries, candidates, loss_weight, positives, shard_row, rows)
    arrived = lax.all_to_all(slots, ("blk", "dp"), split_axis=0, concat_axis=0, tiled=True)
    decoder_grad = pl.pallas_call(
        landing_kernel,
        out_shape=jax.ShapeDtypeStruct((HR, D), F32),
        in_specs=[vmem, vmem],
        out_specs=vmem,
        scratch_shapes=[pltpu.VMEM((4 * HR, 16 * SHARDS), BF16)],
        compiler_params=pltpu.CompilerParams(vmem_limit_bytes=40 * 2**20),
        name="landing",
    )(key, arrived)
    return query_grad, decoder_grad


def solution(mesh):
    return jax.shard_map(
        per_device,
        mesh=mesh,
        in_specs=(
            P("dp", "blk", None),
            P("dp", "blk", None),
            P("dp", "blk"),
            P("dp", "blk"),
            P("dp", "blk", None),
            P("dp", "blk"),
        ),
        out_specs=(P("dp", "blk", None), P(("blk", "dp"), None)),
        check_vma=False,
    )
```

```python
import functools
import math

import jax
import jax.numpy as jnp
from jax import lax
from jax.experimental import pallas as pl
from jax.experimental.pallas import tpu as pltpu
from jax.sharding import PartitionSpec as P

D = 2560
HR = 256
MOST = 4
NQ = 1024
CB = 128
HB = 64
NC = 5
CW = D // NC
SHARDS = 128
SCALE = 1.0 / math.sqrt(D)
F32, BF16, I32 = jnp.float32, jnp.bfloat16, jnp.int32

SELF, XN, ZP, ZM, Z2 = 0, 2, 4, 6, 8
ZPX, ZMX, Z2X = (10, 13), (11, 14), (12, 15)
GROUPS = ((0, 4), (4, 4), (8, 5), (13, 3))

MESSAGES = (
    (0, 2, "x"), (2, 2, "p"), (4, 2, "m"), (6, 1, "p"), (7, 1, "m"),
    (8, 1, "p"), (9, 1, "m"), (10, 2, "x"), (12, 1, "p"), (13, 1, "m"),
)
NM = len(MESSAGES)
KEEP = {SELF: 0, SELF + 1: 1, XN: 2, XN + 1: 3, ZP: 4, ZP + 1: 5, ZM: 6, ZM + 1: 7, Z2: 8, Z2 + 1: 9}
FAR = (2, 1, 3, 0)


def main_kernel(
    q_hbm, c_hbm, w_ref, pos_ref, shard_ref, row_ref, qg_hbm, out_hbm,
    q, c, e, coef_t, coef, prod, snd, rcv, qg, sel, gs, mx, sm, meta, land, out,
    near, cross, from_core, from_x, from_y, from_z,
    q_sem, c_sem, ag_send, ag_recv, rs_send, rs_recv, qg_sem, out_sem,
    meta_send, meta_recv, slot_send, core_recv, x_recv, y_recv, z_recv,
):
    blk, dp = lax.axis_index("blk"), lax.axis_index("dp")
    z, x_lo = lax.div(blk, 2), lax.rem(blk, 2)
    x_hi, y, core = lax.div(dp, 8), lax.rem(lax.div(dp, 2), 4), lax.rem(dp, 2)
    x = x_hi * 2 + x_lo

    def at(dz, dx):
        return lax.rem(z + dz, 4) * 2 + lax.rem(x_lo + dx, 2)

    def device(dz=0, dy=0, dx=0, dc=0):
        across = lax.rem(x + dx, 4)
        return {
            "blk": lax.rem(z + dz, 4) * 2 + lax.rem(across, 2),
            "dp": lax.div(across, 2) * 8 + lax.rem(y + dy, 4) * 2 + lax.rem(core + dc, 2),
        }

    def to(src, dst, send, recv, **way):
        return pltpu.make_async_remote_copy(
            src_ref=src, dst_ref=dst, send_sem=send, recv_sem=recv,
            device_id=device(**way), device_id_type=pl.DeviceIdType.MESH,
        )

    def whole(ref, sem):
        pltpu.make_async_copy(ref, ref, sem).wait()

    peers = {"x": at(0, 1), "p": at(1, 0), "m": at(3, 0)}

    q_copy = pltpu.make_async_copy(q_hbm.at[0], q, q_sem)
    q_copy.start()
    own = [
        pltpu.make_async_copy(c_hbm.at[0, pl.ds(h * HB, HB)], c.at[h], c_sem.at[h]) for h in (0, 1)
    ]
    for copy in own:
        copy.start()

    meta[0, 0, 0, 0, 0:1, :] = shard_ref[...]
    meta[0, 0, 0, 0, 1:2, :] = row_ref[...]
    lines = [{"dc": 1}] + [{axis: far} for axis in ("dx", "dy", "dz") for far in (1, 2, 3)]
    barrier = pltpu.get_barrier_semaphore()
    for line in lines:
        pl.semaphore_signal(
            barrier, inc=1, device_id=device(**line), device_id_type=pl.DeviceIdType.MESH
        )
    pl.semaphore_wait(barrier, len(lines))

    def ag(src, dst, way):
        source = c_hbm.at[0, pl.ds(src * HB, HB)] if src < 2 else c.at[src]
        return pltpu.make_async_remote_copy(
            src_ref=source,
            dst_ref=c.at[dst],
            send_sem=ag_send.at[dst],
            recv_sem=ag_recv.at[dst],
            device_id={"blk": peers[way]},
            device_id_type=pl.DeviceIdType.MESH,
        )

    gather = {
        ZM: ag(0, ZM, "p"), ZP + 1: ag(1, ZP + 1, "m"), XN: ag(0, XN, "x"),
        ZM + 1: ag(1, ZM + 1, "p"), ZP: ag(0, ZP, "m"), XN + 1: ag(1, XN + 1, "x"),
        Z2: ag(ZM, Z2, "p"), Z2 + 1: ag(ZP + 1, Z2 + 1, "m"),
        ZMX[0]: ag(XN, ZMX[0], "p"), ZPX[0]: ag(XN, ZPX[0], "m"),
        ZMX[1]: ag(XN + 1, ZMX[1], "p"), ZPX[1]: ag(XN + 1, ZPX[1], "m"),
        Z2X[0]: ag(Z2, Z2X[0], "x"), Z2X[1]: ag(Z2 + 1, Z2X[1], "x"),
    }
    for slot in (ZM, ZP + 1, XN, ZM + 1, ZP, XN + 1):
        gather[slot].start()

    def tell(k, src, dst, **way):
        return to(src, dst, meta_send.at[k], meta_recv.at[k], **way)

    tell_core = [tell(0, meta.at[0, 0, 0, 0], meta.at[0, 0, 0, 1], dc=1)]
    tell_x = [tell(far, meta.at[0, 0, 0], meta.at[0, 0, far], dx=far) for far in (1, 2, 3)]
    tell_y = [tell(3 + far, meta.at[0, 0], meta.at[0, far], dy=far) for far in (1, 2, 3)]
    tell_z = [tell(6 + far, meta.at[0], meta.at[far], dz=far) for far in (1, 2, 3)]
    for copy in tell_core:
        copy.start()

    shard = shard_ref[...]
    wide = jnp.broadcast_to(shard, (CB, CB))
    earlier = (jnp.transpose(wide) == wide) & (
        lax.broadcasted_iota(I32, (CB, CB), 0) < lax.broadcasted_iota(I32, (CB, CB), 1)
    )
    place = jnp.sum(earlier.astype(I32), axis=0, keepdims=True)
    slot_index = shard * MOST + place
    keys = jnp.concatenate([slot_index * 4 + part for part in range(4)], axis=1)

    def fill(i, _):
        row = i * 256 + lax.broadcasted_iota(I32, (256, 1), 0)
        number = row // 16
        inside = number % 64
        rest = jnp.maximum(inside - 16, 0)
        straight = inside < 16
        dc = (number < 64).astype(I32)
        dz = jnp.where(straight, inside // 4, rest // 12)
        dx = jnp.where(straight, 0, 1 + (rest % 12) // 4)
        across = (x + dx) % 4
        to_shard = ((z + dz) % 4 * 2 + across % 2) * 16 + (
            across // 2 * 8 + (y + inside % 4) % 4 * 2 + (core + dc) % 2
        )
        key = (to_shard * MOST + row % 4) * 4 + (row // 4) % 4
        sel[pl.ds(pl.multiple_of(i * 256, 256), 256), :] = (key == keys).astype(F32).astype(BF16)
        return 0

    lax.fori_loop(0, 16 * SHARDS // 256, fill, 0)
    for copy in tell_core:
        copy.wait_recv()
    for copy in tell_x:
        copy.start()
    q_copy.wait()
    for copy in own:
        copy.wait()

    def scores(which):
        first, number = GROUPS[which]

        def part(i, _):
            span = pl.ds(pl.multiple_of(i * 256, 256), 256)
            s = lax.dot_general(
                c[first : first + number].reshape(number * HB, D), q[span, :],
                (((1,), (1,)), ((), ())), preferred_element_type=F32,
            ) * SCALE
            top = jnp.max(s, axis=0, keepdims=True)
            shifted = jnp.exp(s - top)
            e[first : first + number, :, span] = shifted.reshape(number, HB, 256)
            mx[which : which + 1, span] = top
            sm[which : which + 1, span] = jnp.sum(shifted, axis=0, keepdims=True)
            return 0

        lax.fori_loop(0, NQ // 256, part, 0)

    gather[ZM].wait_recv()
    gather[Z2].start()
    gather[ZP + 1].wait_recv()
    gather[Z2 + 1].start()
    gather[XN].wait_recv()
    gather[XN + 1].wait_recv()
    scores(0)
    for copy in tell_x:
        copy.wait_recv()
    for copy in tell_y:
        copy.start()
    gather[ZM + 1].wait_recv()
    gather[ZP].wait_recv()
    scores(1)
    for copy in tell_y:
        copy.wait_recv()
    for copy in tell_z:
        copy.start()
    gather[Z2].wait_recv()
    gather[Z2X[0]].start()
    gather[Z2 + 1].wait_recv()
    gather[Z2X[1]].start()
    for slot in (ZMX[0], ZPX[0], ZMX[1], ZPX[1]):
        gather[slot].start()
    for slot in (ZPX[0], ZMX[0], Z2X[0]):
        gather[slot].wait_recv()
    scores(2)
    for slot in (ZPX[1], ZMX[1], Z2X[1]):
        gather[slot].wait_recv()
    scores(3)

    top = jnp.max(mx[0:4], axis=0, keepdims=True)
    rescale = jnp.exp(mx[0:4] - top)
    inverse = 1.0 / jnp.sum(rescale * sm[0:4], axis=0, keepdims=True)
    weight, target = w_ref[...], pos_ref[...]
    places = {
        0: at(0, 0), 2: at(0, 1), 4: at(1, 0), 6: at(3, 0), 8: at(2, 0),
    }
    starts = [0] * 16
    for first, owner in places.items():
        starts[first], starts[first + 1] = owner * CB, owner * CB + HB
    for (low, high), owner in ((ZPX, at(1, 1)), (ZMX, at(3, 1)), (Z2X, at(2, 1))):
        starts[low], starts[high] = owner * CB, owner * CB + HB
    for which, (first, number) in enumerate(GROUPS):
        factor = rescale[which : which + 1] * inverse
        for k in range(first, first + number):
            ids = starts[k] + lax.broadcasted_iota(I32, (HB, NQ), 0)
            onehot = (ids == target).astype(F32)
            coef_t[k] = (weight * (e[k] * factor - onehot)).astype(BF16)

    def message(m, chunk):
        first, number, way = MESSAGES[m]
        return pltpu.make_async_remote_copy(
            src_ref=snd.at[chunk, pl.ds(first, number)],
            dst_ref=rcv.at[chunk, pl.ds(first, number)],
            send_sem=rs_send.at[chunk, m],
            recv_sem=rs_recv.at[chunk, m],
            device_id={"blk": peers[way]},
            device_id_type=pl.DeviceIdType.MESH,
        )

    def qg_copy(chunk):
        return pltpu.make_async_copy(
            qg.at[lax.rem(chunk, 2)],
            qg_hbm.at[0, :, pl.ds(pl.multiple_of(chunk * CW, CW), CW)],
            qg_sem.at[lax.rem(chunk, 2)],
        )

    def put(chunk, slot, value):
        snd[chunk, slot] = value.astype(BF16)

    def got(chunk, slot):
        return rcv[chunk, slot].astype(F32)

    def kept(chunk, slot):
        return prod[lax.rem(chunk, 4), KEEP[slot]]

    def core_copies(k):
        send, recv = slot_send.at[k, 0], core_recv
        return [
            to(near.at[k], from_x.at[k, :, 0, 1], send, recv.at[k, 0], dc=1),
            to(cross.at[k], from_core.at[k, :, :, 1], send, recv.at[k, 1], dc=1),
        ]

    def x_leg(k):
        for copy in core_copies(k):
            copy.wait_recv()
        for dz in FAR:
            for far in (1, 2, 3):
                to(from_core.at[k, dz, far - 1], from_x.at[k, dz, far],
                   slot_send.at[k, 1], x_recv.at[k, dz], dx=far).start()

    def y_leg(k, dz):
        whole(from_x.at[k, dz, pl.ds(1, 3)], x_recv.at[k, dz])
        for far in (1, 2, 3):
            to(from_x.at[k, dz, :, :, far], from_y.at[k, dz, far - 1],
               slot_send.at[k, 2], y_recv.at[k, dz], dy=far).start()

    def z_leg(k, dz):
        whole(from_y.at[k, dz], y_recv.at[k, dz])
        if dz:
            to(from_x.at[k, dz, :, :, 0], from_z.at[k, dz - 1, 0],
               slot_send.at[k, 3], z_recv.at[k, dz - 1], dz=dz).start()
            to(from_y.at[k, dz], from_z.at[k, dz - 1, pl.ds(1, 3)],
               slot_send.at[k, 3], z_recv.at[k, dz - 1], dz=dz).start()

    def out_copy(chunk):
        return pltpu.make_async_copy(
            out.at[chunk],
            out_hbm.at[:, pl.ds(pl.multiple_of(chunk * CW, CW), CW)],
            out_sem.at[chunk],
        )

    def touch_down(chunk):
        for dz in (1, 2, 3):
            whole(from_z.at[chunk, dz - 1], z_recv.at[chunk, dz - 1])
        total = jnp.dot(
            land[:, 0:1536], from_z[chunk].reshape(1536, 128), preferred_element_type=F32
        )
        total += jnp.dot(
            land[:, 1536:1920], from_y[chunk, 0].reshape(384, 128), preferred_element_type=F32
        )
        total += jnp.dot(
            land[:, 1920:2048], from_x[chunk, 0, :, :, 0].reshape(128, 128),
            preferred_element_type=F32,
        )
        for part in range(4):
            out[chunk, :, part * 128 : part * 128 + 128] = total[part * HR : part * HR + HR]
        out_copy(chunk).start()

    def landing_rows():
        for copy in tell_z:
            copy.wait_recv()
        everyone = meta[...].reshape(SHARDS, 2, CB)
        order = [everyone[32:128], everyone[8:32], everyone[0:8]]
        shards = jnp.concatenate([part[:, 0, :] for part in order], axis=0)
        numbers = jnp.concatenate([part[:, 1, :] for part in order], axis=0)
        hits = (shards == blk * 16 + dp).astype(F32)
        before = (
            lax.broadcasted_iota(I32, (CB, CB), 0) < lax.broadcasted_iota(I32, (CB, CB), 1)
        ).astype(F32).astype(BF16)
        spot = jnp.dot(hits.astype(BF16), before, preferred_element_type=F32)
        numbers = (numbers + 1).astype(F32) * hits
        lanes = lax.broadcasted_iota(I32, (SHARDS, 16 * SHARDS), 1)
        spread = lanes // 16 == lax.broadcasted_iota(I32, (SHARDS, 16 * SHARDS), 0)
        spread = spread.astype(F32).astype(BF16)
        slot = lax.broadcasted_iota(I32, (8, 16 * SHARDS), 1) % 4
        key = jnp.zeros((8, 16 * SHARDS), F32)
        for k in range(MOST):
            chosen = jnp.where(spot == float(k), numbers, 0.0).astype(BF16)
            by_source = lax.dot_general(
                jnp.ones((8, CB), BF16), chosen, (((1,), (1,)), ((), ())),
                preferred_element_type=F32,
            )
            by_slot = jnp.dot(by_source.astype(BF16), spread, preferred_element_type=F32)
            key = key + jnp.where(slot == k, by_slot, 0.0)
        key = key[0:1].astype(I32) - 1
        part = (lax.broadcasted_iota(I32, (1, 16 * SHARDS), 1) // 4) % 4
        for k in range(4):
            mine = jnp.where(part == k, key, -1)
            for half in range(HR // 64):
                rows = half * 64 + lax.broadcasted_iota(I32, (64, 16 * SHARDS), 0)
                first = k * HR + half * 64
                land[first : first + 64, :] = (rows == mine).astype(F32).astype(BF16)

    def step(i, _):
        @pl.when(i < NC)
        def _():
            slab = lax.rem(i, 4)
            for half in range(CW // 256):
                columns = pl.ds(pl.multiple_of(i * CW + half * 256, 256), 256)
                span = slice(half * 256, half * 256 + 256)
                block = jnp.dot(
                    coef_t[...].reshape(16 * HB, NQ), q[:, columns], preferred_element_type=F32
                ) * SCALE
                block = block.reshape(16, HB, 256)
                for slot, k in KEEP.items():
                    prod[slab, k, :, span] = block[slot]
                for k, slot in enumerate(Z2X + ZPX + ZMX):
                    snd[i, k, :, span] = block[slot].astype(BF16)
                snd[i, 6, :, span] = block[ZP].astype(BF16)
                snd[i, 7, :, span] = block[ZM + 1].astype(BF16)
            for m in range(5):
                message(m, i).start()

        @pl.when((i >= 1) & (i <= NC))
        def _():
            k = i - 1
            message(0, k).wait_recv()
            put(k, 9, kept(k, Z2) + got(k, 0))
            message(6, k).start()
            put(k, 8, kept(k, Z2 + 1) + got(k, 1))
            message(5, k).start()
            message(1, k).wait_recv()
            message(2, k).wait_recv()
            put(k, 10, kept(k, XN) + got(k, 2) + got(k, 4))
            put(k, 11, kept(k, XN + 1) + got(k, 3) + got(k, 5))
            message(7, k).start()

        @pl.when((i >= 2) & (i <= NC + 1))
        def _():
            k = i - 2
            message(5, k).wait_recv()
            put(k, 12, kept(k, ZP + 1) + got(k, 8))
            message(8, k).start()
            message(6, k).wait_recv()
            put(k, 13, kept(k, ZM) + got(k, 9))
            message(9, k).start()

        @pl.when((i >= 3) & (i <= NC + 2))
        def _():
            k = i - 3
            for m in (3, 4, 7, 8, 9):
                message(m, k).wait_recv()
            low = kept(k, SELF) + got(k, 6) + got(k, 13) + got(k, 10)
            high = kept(k, SELF + 1) + got(k, 7) + got(k, 12) + got(k, 11)
            for part in range(4):
                lanes = slice(part * 128, part * 128 + 128)
                gs[part * CB : part * CB + HB, :] = low[:, lanes].astype(BF16)
                gs[part * CB + HB : part * CB + CB, :] = high[:, lanes].astype(BF16)
            picked = jnp.dot(sel[...], gs[...], preferred_element_type=F32).astype(BF16)
            near[k] = picked[0:256].reshape(4, 4, 16, 128)
            cross[k] = picked[256:1024].reshape(4, 3, 4, 16, 128)
            from_x[k, :, 0, 0] = picked[1024:1280].reshape(4, 4, 16, 128)
            from_core[k, :, :, 0] = picked[1280:2048].reshape(4, 3, 4, 16, 128)
            for copy in core_copies(k):
                copy.start()

        @pl.when((i >= 4) & (i <= NC + 3))
        def _():
            x_leg(i - 4)

        @pl.when((i >= 5) & (i <= NC + 4))
        def _():
            for dz in FAR:
                y_leg(i - 5, dz)

        @pl.when((i >= 6) & (i <= NC + 4))
        def _():
            for dz in FAR:
                z_leg(i - 6, dz)

        @pl.when(i == 0)
        def _():
            for k in range(4):
                coef[pl.ds(k * 256, 256), :] = jnp.transpose(
                    coef_t[:, :, k * 256 : k * 256 + 256].reshape(16 * HB, 256)
                )

        @pl.when(i < NC)
        def _():
            @pl.when(i >= 2)
            def _():
                qg_copy(i - 2).wait()

            for half in range(CW // 256):
                columns = pl.ds(pl.multiple_of(i * CW + half * 256, 256), 256)
                total = jnp.dot(
                    coef[...], c[:, :, columns].reshape(16 * HB, 256), preferred_element_type=F32
                )
                qg[lax.rem(i, 2), :, half * 256 : half * 256 + 256] = (total * SCALE).astype(BF16)
            qg_copy(i).start()

        @pl.when(i == 2)
        def _():
            landing_rows()

        @pl.when((i >= 7) & (i <= NC + 4))
        def _():
            touch_down(i - 7)

        return 0

    lax.fori_loop(0, NC + 5, step, 0)
    for dz in FAR:
        z_leg(NC - 1, dz)
    for chunk in (NC - 2, NC - 1):
        touch_down(chunk)

    for copy in gather.values():
        copy.wait_send()

    for copy in tell_core + tell_x + tell_y + tell_z:
        copy.wait_send()

    def drain(i, _):
        for m in range(NM):
            message(m, i).wait_send()
        whole(from_x.at[i, pl.ds(0, 2)], slot_send.at[i, 0])
        whole(from_core.at[i], slot_send.at[i, 1])
        whole(from_y.at[i], slot_send.at[i, 2])
        whole(from_z.at[i], slot_send.at[i, 3])
        out_copy(i).wait()
        return 0

    lax.fori_loop(0, NC, drain, 0)
    qg_copy(NC - 2).wait()
    qg_copy(NC - 1).wait()


def per_device(queries, candidates, loss_weight, positives, producers, rows):
    vmem, hbm = pl.BlockSpec(memory_space=pltpu.VMEM), pl.BlockSpec(memory_space=pl.ANY)
    shard_row = producers.reshape(1, CB)
    return pl.pallas_call(
        main_kernel,
        out_shape=(
            jax.ShapeDtypeStruct((1, NQ, D), BF16),
            jax.ShapeDtypeStruct((HR, D), F32),
        ),
        in_specs=[hbm, hbm, vmem, vmem, vmem, vmem],
        out_specs=(hbm, hbm),
        scratch_shapes=[
            pltpu.VMEM((NQ, D), BF16),
            pltpu.VMEM((16, HB, D), BF16),
            pltpu.VMEM((16, HB, NQ), F32),
            pltpu.VMEM((16, HB, NQ), BF16),
            pltpu.VMEM((NQ, 16 * HB), BF16),
            pltpu.VMEM((4, len(KEEP), HB, CW), F32),
            pltpu.VMEM((NC, 14, HB, CW), BF16),
            pltpu.VMEM((NC, 14, HB, CW), BF16),
            pltpu.VMEM((2, NQ, CW), BF16),
            pltpu.VMEM((16 * SHARDS, 4 * CB), BF16),
            pltpu.VMEM((4 * CB, 128), BF16),
            pltpu.VMEM((8, NQ), F32),
            pltpu.VMEM((8, NQ), F32),
            pltpu.VMEM((4, 4, 4, 2, 2, CB), I32),
            pltpu.VMEM((4 * HR, 16 * SHARDS), BF16),
            pltpu.VMEM((NC, HR, CW), F32),
            pltpu.VMEM((NC, 4, 4, 16, 128), BF16),
            pltpu.VMEM((NC, 4, 3, 4, 16, 128), BF16),
            pltpu.VMEM((NC, 4, 3, 2, 4, 16, 128), BF16),
            pltpu.VMEM((NC, 4, 4, 2, 4, 16, 128), BF16),
            pltpu.VMEM((NC, 4, 3, 4, 2, 16, 128), BF16),
            pltpu.VMEM((NC, 3, 4, 4, 2, 16, 128), BF16),
            pltpu.SemaphoreType.DMA,
            pltpu.SemaphoreType.DMA((2,)),
            pltpu.SemaphoreType.DMA((16,)),
            pltpu.SemaphoreType.DMA((16,)),
            pltpu.SemaphoreType.DMA((NC, NM)),
            pltpu.SemaphoreType.DMA((NC, NM)),
            pltpu.SemaphoreType.DMA((2,)),
            pltpu.SemaphoreType.DMA((NC,)),
            pltpu.SemaphoreType.DMA((10,)),
            pltpu.SemaphoreType.DMA((10,)),
            pltpu.SemaphoreType.DMA((NC, 4)),
            pltpu.SemaphoreType.DMA((NC, 2)),
            pltpu.SemaphoreType.DMA((NC, 4)),
            pltpu.SemaphoreType.DMA((NC, 4)),
            pltpu.SemaphoreType.DMA((NC, 3)),
        ],
        compiler_params=pltpu.CompilerParams(
            collective_id=0, has_side_effects=True, vmem_limit_bytes=62 * 2**20
        ),
        cost_estimate=pl.CostEstimate(
            flops=6 * NQ * NQ * D, bytes_accessed=20 * 2**20, transcendentals=NQ * NQ
        ),
        name="listwise_backward",
    )(queries, candidates, loss_weight, positives, shard_row, rows)


def solution(mesh):
    return jax.shard_map(
        per_device,
        mesh=mesh,
        in_specs=(
            P("dp", "blk", None),
            P("dp", "blk", None),
            P("dp", "blk"),
            P("dp", "blk"),
            P("dp", "blk", None),
            P("dp", "blk"),
        ),
        out_specs=(P("dp", "blk", None), P(("blk", "dp"), None)),
        check_vma=False,
    )
```

```python
import functools
import math

import jax
import jax.numpy as jnp
from jax import lax
from jax.experimental import pallas as pl
from jax.experimental.pallas import tpu as pltpu
from jax.sharding import PartitionSpec as P

D = 2560
HR = 256
MOST = 4
NQ = 1024
CB = 128
HB = 64
NC = 5
CW = D // NC
ND = 5
PER = NC // ND
QW = 512
BW = D // ND // 2
SHARDS = 128
SCALE = 1.0 / math.sqrt(D)
F32, BF16, I32 = jnp.float32, jnp.bfloat16, jnp.int32

SELF, XN, ZP, ZM, Z2 = 0, 2, 4, 6, 8
ZPX, ZMX, Z2X = (10, 13), (11, 14), (12, 15)
GROUPS = ((0, 4), (4, 4), (8, 5), (13, 3))

MESSAGES = (
    (0, 2, "x"), (2, 2, "p"), (4, 2, "m"), (6, 1, "p"), (7, 1, "m"),
    (8, 1, "p"), (9, 1, "m"), (10, 2, "x"), (12, 1, "p"), (13, 1, "m"),
)
NM = len(MESSAGES)
KEEP = {SELF: 0, SELF + 1: 1, XN: 2, XN + 1: 3, ZP: 4, ZP + 1: 5, ZM: 6, ZM + 1: 7, Z2: 8, Z2 + 1: 9}
PAIRS = SHARDS // 2

AWAY = sorted(
    ((n // 16, n // 4 % 4, n % 4) for n in range(1, PAIRS)),
    key=lambda way: -sum(min(far, 4 - far) for far in way),
)


def main_kernel(
    q_hbm, c_hbm, w_ref, pos_ref, shard_ref, row_ref, qg_hbm, out_hbm,
    q, c, e, coef_t, coef, prod, snd, rcv, qg, sel, mx, sm, meta, land, out,
    grad, sent, landed,
    q_sem, c_sem, ag_send, ag_recv, rs_send, rs_recv, qg_sem, out_sem,
    meta_send, meta_recv, core_send, core_recv, slot_send, slot_recv,
):
    blk, dp = lax.axis_index("blk"), lax.axis_index("dp")
    z, x_lo = lax.div(blk, 2), lax.rem(blk, 2)
    x_hi, y, core = lax.div(dp, 8), lax.rem(lax.div(dp, 2), 4), lax.rem(dp, 2)
    x = x_hi * 2 + x_lo

    def at(dz, dx):
        return lax.rem(z + dz, 4) * 2 + lax.rem(x_lo + dx, 2)

    def device(dz=0, dy=0, dx=0, dc=0):
        across = lax.rem(x + dx, 4)
        return {
            "blk": lax.rem(z + dz, 4) * 2 + lax.rem(across, 2),
            "dp": lax.div(across, 2) * 8 + lax.rem(y + dy, 4) * 2 + lax.rem(core + dc, 2),
        }

    def to(src, dst, send, recv, **way):
        return pltpu.make_async_remote_copy(
            src_ref=src, dst_ref=dst, send_sem=send, recv_sem=recv,
            device_id=device(**way), device_id_type=pl.DeviceIdType.MESH,
        )

    def whole(ref, sem):
        pltpu.make_async_copy(ref, ref, sem).wait()

    peers = {"x": at(0, 1), "p": at(1, 0), "m": at(3, 0)}

    q_copy = pltpu.make_async_copy(q_hbm.at[0], q, q_sem)
    q_copy.start()
    own = [
        pltpu.make_async_copy(c_hbm.at[0, pl.ds(h * HB, HB)], c.at[h], c_sem.at[h]) for h in (0, 1)
    ]
    for copy in own:
        copy.start()

    meta[0, 0, 0, 0, 0:1, :] = shard_ref[...]
    meta[0, 0, 0, 0, 1:2, :] = row_ref[...]
    lines = [{"dc": 1}] + [{"dz": dz, "dy": dy, "dx": dx} for dz, dy, dx in AWAY]
    barrier = pltpu.get_barrier_semaphore()
    for line in lines:
        pl.semaphore_signal(
            barrier, inc=1, device_id=device(**line), device_id_type=pl.DeviceIdType.MESH
        )
    pl.semaphore_wait(barrier, len(lines))

    def ag(src, dst, way):
        source = c_hbm.at[0, pl.ds(src * HB, HB)] if src < 2 else c.at[src]
        return pltpu.make_async_remote_copy(
            src_ref=source,
            dst_ref=c.at[dst],
            send_sem=ag_send.at[dst],
            recv_sem=ag_recv.at[dst],
            device_id={"blk": peers[way]},
            device_id_type=pl.DeviceIdType.MESH,
        )

    gather = {
        ZM: ag(0, ZM, "p"), ZP + 1: ag(1, ZP + 1, "m"), XN: ag(0, XN, "x"),
        ZM + 1: ag(1, ZM + 1, "p"), ZP: ag(0, ZP, "m"), XN + 1: ag(1, XN + 1, "x"),
        Z2: ag(ZM, Z2, "p"), Z2 + 1: ag(ZP + 1, Z2 + 1, "m"),
        ZMX[0]: ag(XN, ZMX[0], "p"), ZPX[0]: ag(XN, ZPX[0], "m"),
        ZMX[1]: ag(XN + 1, ZMX[1], "p"), ZPX[1]: ag(XN + 1, ZPX[1], "m"),
        Z2X[0]: ag(Z2, Z2X[0], "x"), Z2X[1]: ag(Z2 + 1, Z2X[1], "x"),
    }
    for slot in (ZM, ZP + 1, XN, ZM + 1, ZP, XN + 1):
        gather[slot].start()

    def tell(k, src, dst, **way):
        return to(src, dst, meta_send.at[k], meta_recv.at[k], **way)

    tell_core = [tell(0, meta.at[0, 0, 0, 0], meta.at[0, 0, 0, 1], dc=1)]
    tell_x = [tell(far, meta.at[0, 0, 0], meta.at[0, 0, far], dx=far) for far in (1, 2, 3)]
    tell_y = [tell(3 + far, meta.at[0, 0], meta.at[0, far], dy=far) for far in (1, 2, 3)]
    tell_z = [tell(6 + far, meta.at[0], meta.at[far], dz=far) for far in (1, 2, 3)]
    for copy in tell_core:
        copy.start()

    for copy in tell_core:
        copy.wait_recv()
    for copy in tell_x:
        copy.start()

    keys = []
    for chip_core in range(2):
        shard = meta[0, 0, 0, chip_core, 0:1, :]
        wide = jnp.broadcast_to(shard, (CB, CB))
        earlier = (jnp.transpose(wide) == wide) & (
            lax.broadcasted_iota(I32, (CB, CB), 0) < lax.broadcasted_iota(I32, (CB, CB), 1)
        )
        place = jnp.sum(earlier.astype(I32), axis=0, keepdims=True)
        keys.append((shard * MOST + place) * 4 + chip_core * 2)
    keys = jnp.concatenate([keys[0], keys[1], keys[0] + 1, keys[1] + 1], axis=1)

    def fill(i, _):
        row = i * 256 + lax.broadcasted_iota(I32, (256, 1), 0)
        block = row // 16
        across = (x + block % 4) % 4
        to_shard = ((z + block // 16) % 4 * 2 + across % 2) * 16 + (
            across // 2 * 8 + (y + block // 4 % 4) % 4 * 2 + core
        )
        key = (to_shard * MOST + row % 4) * 4 + row // 4 % 4
        sel[pl.ds(pl.multiple_of(i * 256, 256), 256), :] = (key == keys).astype(F32).astype(BF16)
        return 0

    lax.fori_loop(0, 16 * PAIRS // 256, fill, 0)
    q_copy.wait()
    for copy in own:
        copy.wait()

    def scores(which):
        first, number = GROUPS[which]

        def part(i, _):
            span = pl.ds(pl.multiple_of(i * 256, 256), 256)
            s = lax.dot_general(
                c[first : first + number].reshape(number * HB, D), q[span, :],
                (((1,), (1,)), ((), ())), preferred_element_type=F32,
            ) * SCALE
            top = jnp.max(s, axis=0, keepdims=True)
            shifted = jnp.exp(s - top)
            e[first : first + number, :, span] = shifted.reshape(number, HB, 256)
            mx[which : which + 1, span] = top
            sm[which : which + 1, span] = jnp.sum(shifted, axis=0, keepdims=True)
            return 0

        lax.fori_loop(0, NQ // 256, part, 0)

    def landing_rows():
        for copy in tell_z:
            copy.wait_recv()
        everyone = meta[...].reshape(SHARDS, 2, CB)
        shards, numbers = everyone[:, 0, :], everyone[:, 1, :]
        hits = (shards == blk * 16 + dp).astype(F32)
        before = (
            lax.broadcasted_iota(I32, (CB, CB), 0) < lax.broadcasted_iota(I32, (CB, CB), 1)
        ).astype(F32).astype(BF16)
        spot = jnp.dot(hits.astype(BF16), before, preferred_element_type=F32)
        numbers = (numbers + 1).astype(F32) * hits
        lanes = lax.broadcasted_iota(I32, (SHARDS, 8 * SHARDS), 1)
        spread = lanes // 8 == lax.broadcasted_iota(I32, (SHARDS, 8 * SHARDS), 0)
        spread = spread.astype(F32).astype(BF16)
        slot = lax.broadcasted_iota(I32, (8, 8 * SHARDS), 1) % 4
        key = jnp.zeros((8, 8 * SHARDS), F32)
        for k in range(MOST):
            chosen = jnp.where(spot == float(k), numbers, 0.0).astype(BF16)
            by_source = lax.dot_general(
                jnp.ones((8, CB), BF16), chosen, (((1,), (1,)), ((), ())),
                preferred_element_type=F32,
            )
            by_slot = jnp.dot(by_source.astype(BF16), spread, preferred_element_type=F32)
            key = key + jnp.where(slot == k, by_slot, 0.0)
        key = key[0:1].astype(I32) - 1
        part = lax.broadcasted_iota(I32, (1, 8 * SHARDS), 1) // 4 % 2
        for k in range(2):
            mine = jnp.where(part == k, key, -1)
            for piece in range(HR // 64):
                rows = piece * 64 + lax.broadcasted_iota(I32, (64, 8 * SHARDS), 0)
                first = k * HR + piece * 64
                land[first : first + 64, :] = (rows == mine).astype(F32).astype(BF16)

    gather[ZM].wait_recv()
    gather[Z2].start()
    gather[ZP + 1].wait_recv()
    gather[Z2 + 1].start()
    gather[XN].wait_recv()
    gather[XN + 1].wait_recv()
    scores(0)
    for copy in tell_x:
        copy.wait_recv()
    for copy in tell_y:
        copy.start()
    gather[ZM + 1].wait_recv()
    gather[ZP].wait_recv()
    scores(1)
    for copy in tell_y:
        copy.wait_recv()
    for copy in tell_z:
        copy.start()
    gather[Z2].wait_recv()
    gather[Z2X[0]].start()
    gather[Z2 + 1].wait_recv()
    gather[Z2X[1]].start()
    for slot in (ZMX[0], ZPX[0], ZMX[1], ZPX[1]):
        gather[slot].start()
    landing_rows()
    for slot in (ZPX[0], ZMX[0], Z2X[0]):
        gather[slot].wait_recv()
    scores(2)
    for slot in (ZPX[1], ZMX[1], Z2X[1]):
        gather[slot].wait_recv()
    scores(3)

    top = jnp.max(mx[0:4], axis=0, keepdims=True)
    rescale = jnp.exp(mx[0:4] - top)
    inverse = 1.0 / jnp.sum(rescale * sm[0:4], axis=0, keepdims=True)
    weight, target = w_ref[...], pos_ref[...]
    places = {
        0: at(0, 0), 2: at(0, 1), 4: at(1, 0), 6: at(3, 0), 8: at(2, 0),
    }
    starts = [0] * 16
    for first, owner in places.items():
        starts[first], starts[first + 1] = owner * CB, owner * CB + HB
    for (low, high), owner in ((ZPX, at(1, 1)), (ZMX, at(3, 1)), (Z2X, at(2, 1))):
        starts[low], starts[high] = owner * CB, owner * CB + HB
    for which, (first, number) in enumerate(GROUPS):
        factor = rescale[which : which + 1] * inverse
        for k in range(first, first + number):
            ids = starts[k] + lax.broadcasted_iota(I32, (HB, NQ), 0)
            onehot = (ids == target).astype(F32)
            coef_t[k] = (weight * (e[k] * factor - onehot)).astype(BF16)

    def message(m, chunk):
        first, number, way = MESSAGES[m]
        return pltpu.make_async_remote_copy(
            src_ref=snd.at[chunk, pl.ds(first, number)],
            dst_ref=rcv.at[chunk, pl.ds(first, number)],
            send_sem=rs_send.at[chunk, m],
            recv_sem=rs_recv.at[chunk, m],
            device_id={"blk": peers[way]},
            device_id_type=pl.DeviceIdType.MESH,
        )

    def qg_copy(chunk):
        return pltpu.make_async_copy(
            qg.at[lax.rem(chunk, 2)],
            qg_hbm.at[0, :, pl.ds(pl.multiple_of(chunk * QW, QW), QW)],
            qg_sem.at[lax.rem(chunk, 2)],
        )

    def put(chunk, slot, value):
        snd[chunk, slot] = value.astype(BF16)

    def got(chunk, slot):
        return rcv[chunk, slot].astype(F32)

    def kept(chunk, slot):
        return prod[lax.rem(chunk, 4), KEEP[slot]]

    def core_copy(k):
        return to(grad.at[k, 0], grad.at[k, 1], core_send.at[k], core_recv.at[k], dc=1)

    def dispatch(k):
        parts = []
        for chunk in range(PER):
            core_copy(k * PER + chunk).wait_recv()
        for part in range(2):
            for chip_core in range(2):
                first = part * BW
                while first < part * BW + BW:
                    width = min(BW, CW - first % CW)
                    parts.append(grad[k * PER + first // CW, chip_core, :, first % CW : first % CW + width])
                    first += width
        assert len(parts) == 4
        rows = jnp.concatenate(parts, axis=0)
        slots = jnp.dot(sel[...], rows, preferred_element_type=F32).astype(BF16)
        sent[k] = slots.reshape(PAIRS, 16, BW)
        landed[k, 0] = slots[0:16]
        for dz, dy, dx in AWAY:
            n = dz * 16 + dy * 4 + dx
            to(sent.at[k, n], landed.at[k, n], slot_send.at[k], slot_recv.at[k],
               dz=dz, dy=dy, dx=dx).start()

    def out_copy(chunk):
        return pltpu.make_async_copy(
            out.at[chunk],
            out_hbm.at[:, pl.ds(pl.multiple_of(chunk * 2 * BW, 2 * BW), 2 * BW)],
            out_sem.at[chunk],
        )

    def touch_down(k):
        whole(landed.at[k, pl.ds(1, PAIRS - 1)], slot_recv.at[k])
        total = jnp.dot(
            land[...], landed[k].reshape(16 * PAIRS, BW), preferred_element_type=F32
        )
        for part in range(2):
            out[k, :, part * BW : part * BW + BW] = total[part * HR : part * HR + HR]
        out_copy(k).start()

    def step(i, _):
        @pl.when(i < NC)
        def _():
            slab = lax.rem(i, 4)
            columns = pl.ds(pl.multiple_of(i * CW, CW), CW)
            block = jnp.dot(
                coef_t[...].reshape(16 * HB, NQ), q[:, columns], preferred_element_type=F32
            ) * SCALE
            block = block.reshape(16, HB, CW)
            for slot, k in KEEP.items():
                prod[slab, k] = block[slot]
            for k, slot in enumerate(Z2X + ZPX + ZMX + (ZP, ZM + 1)):
                put(i, k, block[slot])
            for m in range(5):
                message(m, i).start()

        @pl.when((i >= 1) & (i <= NC))
        def _():
            k = i - 1
            message(0, k).wait_recv()
            put(k, 9, kept(k, Z2) + got(k, 0))
            message(6, k).start()
            put(k, 8, kept(k, Z2 + 1) + got(k, 1))
            message(5, k).start()
            message(1, k).wait_recv()
            message(2, k).wait_recv()
            put(k, 10, kept(k, XN) + got(k, 2) + got(k, 4))
            put(k, 11, kept(k, XN + 1) + got(k, 3) + got(k, 5))
            message(7, k).start()

        @pl.when((i >= 2) & (i <= NC + 1))
        def _():
            k = i - 2
            message(5, k).wait_recv()
            put(k, 12, kept(k, ZP + 1) + got(k, 8))
            message(8, k).start()
            message(6, k).wait_recv()
            put(k, 13, kept(k, ZM) + got(k, 9))
            message(9, k).start()

        @pl.when((i >= 3) & (i <= NC + 2))
        def _():
            k = i - 3
            for m in (3, 4, 7, 8, 9):
                message(m, k).wait_recv()
            low = kept(k, SELF) + got(k, 6) + got(k, 13) + got(k, 10)
            high = kept(k, SELF + 1) + got(k, 7) + got(k, 12) + got(k, 11)
            grad[k, 0, 0:HB] = low.astype(BF16)
            grad[k, 0, HB:CB] = high.astype(BF16)
            core_copy(k).start()

        @pl.when((i >= 3 + PER) & (lax.rem(i - 3, PER) == 0))
        def _():
            dispatch(lax.div(i - 3, PER) - 1)

        @pl.when(i == NC - 1)
        def _():
            for k in range(4):
                coef[pl.ds(k * 256, 256), :] = jnp.transpose(
                    coef_t[:, :, k * 256 : k * 256 + 256].reshape(16 * HB, 256)
                )

        @pl.when(i >= NC - 1)
        def _():
            query_part(i - (NC - 1))

        return 0

    def query_part(k):
        @pl.when(k >= 2)
        def _():
            qg_copy(k - 2).wait()

        for half in range(QW // 256):
            columns = pl.ds(pl.multiple_of(k * QW + half * 256, 256), 256)
            total = jnp.dot(
                coef[...], c[:, :, columns].reshape(16 * HB, 256), preferred_element_type=F32
            )
            qg[lax.rem(k, 2), :, half * 256 : half * 256 + 256] = (total * SCALE).astype(BF16)
        qg_copy(k).start()

    lax.fori_loop(0, NC + 4, step, 0)

    def land_part(k, _):
        touch_down(k)
        return 0

    lax.fori_loop(0, ND, land_part, 0)

    for copy in gather.values():
        copy.wait_send()

    for copy in tell_core + tell_x + tell_y + tell_z:
        copy.wait_send()

    def drain(i, _):
        for m in range(NM):
            message(m, i).wait_send()
        core_copy(i).wait_send()
        return 0

    lax.fori_loop(0, NC, drain, 0)
    for k in range(ND):
        whole(sent.at[k, pl.ds(1, PAIRS - 1)], slot_send.at[k])
        out_copy(k).wait()
    qg_copy(D // QW - 2).wait()
    qg_copy(D // QW - 1).wait()


def per_device(queries, candidates, loss_weight, positives, producers, rows):
    vmem, hbm = pl.BlockSpec(memory_space=pltpu.VMEM), pl.BlockSpec(memory_space=pl.ANY)
    shard_row = producers.reshape(1, CB)
    return pl.pallas_call(
        main_kernel,
        out_shape=(
            jax.ShapeDtypeStruct((1, NQ, D), BF16),
            jax.ShapeDtypeStruct((HR, D), F32),
        ),
        in_specs=[hbm, hbm, vmem, vmem, vmem, vmem],
        out_specs=(hbm, hbm),
        scratch_shapes=[
            pltpu.VMEM((NQ, D), BF16),
            pltpu.VMEM((16, HB, D), BF16),
            pltpu.VMEM((16, HB, NQ), F32),
            pltpu.VMEM((16, HB, NQ), BF16),
            pltpu.VMEM((NQ, 16 * HB), BF16),
            pltpu.VMEM((4, len(KEEP), HB, CW), F32),
            pltpu.VMEM((NC, 14, HB, CW), BF16),
            pltpu.VMEM((NC, 14, HB, CW), BF16),
            pltpu.VMEM((2, NQ, QW), BF16),
            pltpu.VMEM((16 * PAIRS, 4 * CB), BF16),
            pltpu.VMEM((8, NQ), F32),
            pltpu.VMEM((8, NQ), F32),
            pltpu.VMEM((4, 4, 4, 2, 2, CB), I32),
            pltpu.VMEM((2 * HR, 8 * SHARDS), BF16),
            pltpu.VMEM((ND, HR, 2 * BW), F32),
            pltpu.VMEM((NC, 2, CB, CW), BF16),
            pltpu.VMEM((ND, PAIRS, 16, BW), BF16),
            pltpu.VMEM((ND, PAIRS, 16, BW), BF16),
            pltpu.SemaphoreType.DMA,
            pltpu.SemaphoreType.DMA((2,)),
            pltpu.SemaphoreType.DMA((16,)),
            pltpu.SemaphoreType.DMA((16,)),
            pltpu.SemaphoreType.DMA((NC, NM)),
            pltpu.SemaphoreType.DMA((NC, NM)),
            pltpu.SemaphoreType.DMA((2,)),
            pltpu.SemaphoreType.DMA((ND,)),
            pltpu.SemaphoreType.DMA((10,)),
            pltpu.SemaphoreType.DMA((10,)),
            pltpu.SemaphoreType.DMA((NC,)),
            pltpu.SemaphoreType.DMA((NC,)),
            pltpu.SemaphoreType.DMA((ND,)),
            pltpu.SemaphoreType.DMA((ND,)),
        ],
        compiler_params=pltpu.CompilerParams(
            collective_id=0, has_side_effects=True, vmem_limit_bytes=62 * 2**20
        ),
        cost_estimate=pl.CostEstimate(
            flops=6 * NQ * NQ * D, bytes_accessed=20 * 2**20, transcendentals=NQ * NQ
        ),
        name="listwise_backward",
    )(queries, candidates, loss_weight, positives, shard_row, rows)


def solution(mesh):
    return jax.shard_map(
        per_device,
        mesh=mesh,
        in_specs=(
            P("dp", "blk", None),
            P("dp", "blk", None),
            P("dp", "blk"),
            P("dp", "blk"),
            P("dp", "blk", None),
            P("dp", "blk"),
        ),
        out_specs=(P("dp", "blk", None), P(("blk", "dp"), None)),
        check_vma=False,
    )
```

```python
import functools
import math

import jax
import jax.numpy as jnp
from jax import lax
from jax.experimental import pallas as pl
from jax.experimental.pallas import tpu as pltpu
from jax.sharding import PartitionSpec as P

D = 2560
HR = 256
MOST = 4
NQ = 1024
CB = 128
HB = 64
STAY = 48
NC = 5
CW = D // NC
ND = 5
PER = NC // ND
QW = 512
BW = D // ND // 2
SHARDS = 128
SCALE = 1.0 / math.sqrt(D)
F32, BF16, I32 = jnp.float32, jnp.bfloat16, jnp.int32

SELF, XN, ZP, ZM, Z2 = 0, 2, 4, 6, 8
ZPX, ZMX, Z2X = (10, 13), (11, 14), (12, 15)
GROUPS = ((0, 4), (4, 4), (8, 5), (13, 3))

MESSAGES = (
    (0, 128, "x"), (128, 64 + STAY, "p"), (256, 64 + STAY, "m"), (384, 64, "p"), (448, 64, "m"),
    (512, 64, "p"), (576, 64, "m"), (640, 128, "x"), (768, 64, "p"), (832, 64, "m"),
    (192 + STAY, 64 - STAY, "x"), (320 + STAY, 64 - STAY, "x"),
)
NM = len(MESSAGES)
KEEP = {SELF: 0, SELF + 1: 1, XN: 2, XN + 1: 3, ZP: 4, ZP + 1: 5, ZM: 6, ZM + 1: 7, Z2: 8, Z2 + 1: 9}
PAIRS = SHARDS // 2

AWAY = sorted(
    ((n // 16, n // 4 % 4, n % 4) for n in range(1, PAIRS)),
    key=lambda way: -sum(min(far, 4 - far) for far in way),
)


def main_kernel(
    q_hbm, c_hbm, w_ref, pos_ref, shard_ref, row_ref, qg_hbm, out_hbm,
    q, c, e, coef_t, coef, prod, snd, rcv, qg, sel, mx, sm, meta, land, out,
    grad, sent, landed,
    q_sem, c_sem, ag_send, ag_recv, rs_send, rs_recv, qg_sem, out_sem,
    meta_send, meta_recv, core_send, core_recv, slot_send, slot_recv,
):
    blk, dp = lax.axis_index("blk"), lax.axis_index("dp")
    z, x_lo = lax.div(blk, 2), lax.rem(blk, 2)
    x_hi, y, core = lax.div(dp, 8), lax.rem(lax.div(dp, 2), 4), lax.rem(dp, 2)
    x = x_hi * 2 + x_lo

    def at(dz, dx):
        return lax.rem(z + dz, 4) * 2 + lax.rem(x_lo + dx, 2)

    def device(dz=0, dy=0, dx=0, dc=0):
        across = lax.rem(x + dx, 4)
        return {
            "blk": lax.rem(z + dz, 4) * 2 + lax.rem(across, 2),
            "dp": lax.div(across, 2) * 8 + lax.rem(y + dy, 4) * 2 + lax.rem(core + dc, 2),
        }

    def to(src, dst, send, recv, **way):
        return pltpu.make_async_remote_copy(
            src_ref=src, dst_ref=dst, send_sem=send, recv_sem=recv,
            device_id=device(**way), device_id_type=pl.DeviceIdType.MESH,
        )

    def whole(ref, sem):
        pltpu.make_async_copy(ref, ref, sem).wait()

    peers = {"x": at(0, 1), "p": at(1, 0), "m": at(3, 0)}

    q_copy = pltpu.make_async_copy(q_hbm.at[0], q, q_sem)
    q_copy.start()
    own = [
        pltpu.make_async_copy(c_hbm.at[0, pl.ds(h * HB, HB)], c.at[h], c_sem.at[h]) for h in (0, 1)
    ]
    for copy in own:
        copy.start()

    meta[0, 0, 0, 0, 0:1, :] = shard_ref[...]
    meta[0, 0, 0, 0, 1:2, :] = row_ref[...]
    lines = [{"dc": 1}] + [{"dz": dz, "dy": dy, "dx": dx} for dz, dy, dx in AWAY]
    barrier = pltpu.get_barrier_semaphore()
    for line in lines:
        pl.semaphore_signal(
            barrier, inc=1, device_id=device(**line), device_id_type=pl.DeviceIdType.MESH
        )
    pl.semaphore_wait(barrier, len(lines))

    def ag(src, dst, way, first=0, number=HB, sem=None):
        if src < 2:
            source = c_hbm.at[0, pl.ds(src * HB + first, number)]
        else:
            source = c.at[src, pl.ds(first, number)]
        sem = dst if sem is None else sem
        return pltpu.make_async_remote_copy(
            src_ref=source,
            dst_ref=c.at[dst, pl.ds(first, number)],
            send_sem=ag_send.at[sem],
            recv_sem=ag_recv.at[sem],
            device_id={"blk": peers[way]},
            device_id_type=pl.DeviceIdType.MESH,
        )

    gather = {
        ZM: ag(0, ZM, "p"), ZP + 1: ag(1, ZP + 1, "m"), XN: ag(0, XN, "x"),
        ZM + 1: ag(1, ZM + 1, "p"), ZP: ag(0, ZP, "m"), XN + 1: ag(1, XN + 1, "x"),
        Z2: ag(ZM, Z2, "p"), Z2 + 1: ag(ZP + 1, Z2 + 1, "m"),
        ZMX[0]: ag(XN, ZMX[0], "p"), ZPX[0]: ag(XN, ZPX[0], "m"),
        ZMX[1]: ag(XN + 1, ZMX[1], "p", 0, STAY), ZPX[1]: ag(XN + 1, ZPX[1], "m", 0, STAY),
        16: ag(ZM + 1, ZMX[1], "x", STAY, HB - STAY, 16),
        17: ag(ZP + 1, ZPX[1], "x", STAY, HB - STAY, 17),
        Z2X[0]: ag(Z2, Z2X[0], "x"), Z2X[1]: ag(Z2 + 1, Z2X[1], "x"),
    }
    for slot in (ZM, ZP + 1, XN, ZM + 1, ZP, XN + 1):
        gather[slot].start()

    def tell(k, src, dst, **way):
        return to(src, dst, meta_send.at[k], meta_recv.at[k], **way)

    tell_core = [tell(0, meta.at[0, 0, 0, 0], meta.at[0, 0, 0, 1], dc=1)]
    tell_x = [tell(far, meta.at[0, 0, 0], meta.at[0, 0, far], dx=far) for far in (1, 2, 3)]
    tell_y = [tell(3 + far, meta.at[0, 0], meta.at[0, far], dy=far) for far in (1, 2, 3)]
    tell_z = [tell(6 + far, meta.at[0], meta.at[far], dz=far) for far in (1, 2, 3)]
    for copy in tell_core:
        copy.start()

    for copy in tell_core:
        copy.wait_recv()
    for copy in tell_x:
        copy.start()

    keys = []
    for chip_core in range(2):
        shard = meta[0, 0, 0, chip_core, 0:1, :]
        wide = jnp.broadcast_to(shard, (CB, CB))
        earlier = (jnp.transpose(wide) == wide) & (
            lax.broadcasted_iota(I32, (CB, CB), 0) < lax.broadcasted_iota(I32, (CB, CB), 1)
        )
        place = jnp.sum(earlier.astype(I32), axis=0, keepdims=True)
        keys.append((shard * MOST + place) * 4 + chip_core * 2)
    keys = jnp.concatenate([keys[0], keys[1], keys[0] + 1, keys[1] + 1], axis=1)

    def fill(i, _):
        row = i * 256 + lax.broadcasted_iota(I32, (256, 1), 0)
        block = row // 16
        across = (x + block % 4) % 4
        to_shard = ((z + block // 16) % 4 * 2 + across % 2) * 16 + (
            across // 2 * 8 + (y + block // 4 % 4) % 4 * 2 + core
        )
        key = (to_shard * MOST + row % 4) * 4 + row // 4 % 4
        sel[pl.ds(pl.multiple_of(i * 256, 256), 256), :] = (key == keys).astype(F32).astype(BF16)
        return 0

    lax.fori_loop(0, 16 * PAIRS // 256, fill, 0)
    q_copy.wait()
    for copy in own:
        copy.wait()

    def scores(which):
        first, number = GROUPS[which]

        def part(i, _):
            span = pl.ds(pl.multiple_of(i * 256, 256), 256)
            s = lax.dot_general(
                c[first : first + number].reshape(number * HB, D), q[span, :],
                (((1,), (1,)), ((), ())), preferred_element_type=F32,
            ) * SCALE
            top = jnp.max(s, axis=0, keepdims=True)
            shifted = jnp.exp(s - top)
            e[first : first + number, :, span] = shifted.reshape(number, HB, 256)
            mx[which : which + 1, span] = top
            sm[which : which + 1, span] = jnp.sum(shifted, axis=0, keepdims=True)
            return 0

        lax.fori_loop(0, NQ // 256, part, 0)

    def landing_rows():
        for copy in tell_z:
            copy.wait_recv()
        everyone = meta[...].reshape(SHARDS, 2, CB)
        shards, numbers = everyone[:, 0, :], everyone[:, 1, :]
        hits = (shards == blk * 16 + dp).astype(F32)
        before = (
            lax.broadcasted_iota(I32, (CB, CB), 0) < lax.broadcasted_iota(I32, (CB, CB), 1)
        ).astype(F32).astype(BF16)
        spot = jnp.dot(hits.astype(BF16), before, preferred_element_type=F32)
        numbers = (numbers + 1).astype(F32) * hits
        lanes = lax.broadcasted_iota(I32, (SHARDS, 8 * SHARDS), 1)
        spread = lanes // 8 == lax.broadcasted_iota(I32, (SHARDS, 8 * SHARDS), 0)
        spread = spread.astype(F32).astype(BF16)
        slot = lax.broadcasted_iota(I32, (8, 8 * SHARDS), 1) % 4
        key = jnp.zeros((8, 8 * SHARDS), F32)
        for k in range(MOST):
            chosen = jnp.where(spot == float(k), numbers, 0.0).astype(BF16)
            by_source = lax.dot_general(
                jnp.ones((8, CB), BF16), chosen, (((1,), (1,)), ((), ())),
                preferred_element_type=F32,
            )
            by_slot = jnp.dot(by_source.astype(BF16), spread, preferred_element_type=F32)
            key = key + jnp.where(slot == k, by_slot, 0.0)
        key = key[0:1].astype(I32) - 1
        part = lax.broadcasted_iota(I32, (1, 8 * SHARDS), 1) // 4 % 2
        for k in range(2):
            mine = jnp.where(part == k, key, -1)
            for piece in range(HR // 64):
                rows = piece * 64 + lax.broadcasted_iota(I32, (64, 8 * SHARDS), 0)
                first = k * HR + piece * 64
                land[first : first + 64, :] = (rows == mine).astype(F32).astype(BF16)

    gather[ZM].wait_recv()
    gather[Z2].start()
    gather[ZP + 1].wait_recv()
    gather[Z2 + 1].start()
    gather[XN].wait_recv()
    gather[XN + 1].wait_recv()
    scores(0)
    for copy in tell_x:
        copy.wait_recv()
    for copy in tell_y:
        copy.start()
    gather[17].start()
    gather[ZM + 1].wait_recv()
    gather[16].start()
    gather[ZP].wait_recv()
    scores(1)
    for copy in tell_y:
        copy.wait_recv()
    for copy in tell_z:
        copy.start()
    gather[Z2].wait_recv()
    gather[Z2X[0]].start()
    gather[Z2 + 1].wait_recv()
    gather[Z2X[1]].start()
    for slot in (ZMX[0], ZPX[0], ZMX[1], ZPX[1]):
        gather[slot].start()
    landing_rows()
    for slot in (ZPX[0], ZMX[0], Z2X[0]):
        gather[slot].wait_recv()
    scores(2)
    for slot in (ZPX[1], ZMX[1], 16, 17, Z2X[1]):
        gather[slot].wait_recv()
    scores(3)

    top = jnp.max(mx[0:4], axis=0, keepdims=True)
    rescale = jnp.exp(mx[0:4] - top)
    inverse = 1.0 / jnp.sum(rescale * sm[0:4], axis=0, keepdims=True)
    weight, target = w_ref[...], pos_ref[...]
    places = {
        0: at(0, 0), 2: at(0, 1), 4: at(1, 0), 6: at(3, 0), 8: at(2, 0),
    }
    starts = [0] * 16
    for first, owner in places.items():
        starts[first], starts[first + 1] = owner * CB, owner * CB + HB
    for (low, high), owner in ((ZPX, at(1, 1)), (ZMX, at(3, 1)), (Z2X, at(2, 1))):
        starts[low], starts[high] = owner * CB, owner * CB + HB
    for which, (first, number) in enumerate(GROUPS):
        factor = rescale[which : which + 1] * inverse
        for k in range(first, first + number):
            ids = starts[k] + lax.broadcasted_iota(I32, (HB, NQ), 0)
            onehot = (ids == target).astype(F32)
            coef_t[k] = (weight * (e[k] * factor - onehot)).astype(BF16)

    def message(m, chunk):
        first, number, way = MESSAGES[m]
        return pltpu.make_async_remote_copy(
            src_ref=snd.at[chunk, pl.ds(first, number)],
            dst_ref=rcv.at[chunk, pl.ds(first, number)],
            send_sem=rs_send.at[chunk, m],
            recv_sem=rs_recv.at[chunk, m],
            device_id={"blk": peers[way]},
            device_id_type=pl.DeviceIdType.MESH,
        )

    def qg_copy(chunk):
        return pltpu.make_async_copy(
            qg.at[lax.rem(chunk, 2)],
            qg_hbm.at[0, :, pl.ds(pl.multiple_of(chunk * QW, QW), QW)],
            qg_sem.at[lax.rem(chunk, 2)],
        )

    def put(chunk, slot, value):
        snd[chunk, slot * HB : slot * HB + HB] = value.astype(BF16)

    def got(chunk, slot):
        return rcv[chunk, slot * HB : slot * HB + HB].astype(F32)

    def by_z(chunk, slot):
        return jnp.where(lax.broadcasted_iota(I32, (HB, CW), 0) < STAY, got(chunk, slot), 0.0)

    def by_x(chunk, slot):
        return jnp.where(lax.broadcasted_iota(I32, (HB, CW), 0) >= STAY, got(chunk, slot), 0.0)

    def kept(chunk, slot):
        return prod[lax.rem(chunk, 4), KEEP[slot]]

    def core_copy(k):
        return to(grad.at[k, 0], grad.at[k, 1], core_send.at[k], core_recv.at[k], dc=1)

    def dispatch(k):
        parts = []
        for chunk in range(PER):
            core_copy(k * PER + chunk).wait_recv()
        for part in range(2):
            for chip_core in range(2):
                first = part * BW
                while first < part * BW + BW:
                    width = min(BW, CW - first % CW)
                    parts.append(grad[k * PER + first // CW, chip_core, :, first % CW : first % CW + width])
                    first += width
        assert len(parts) == 4
        rows = jnp.concatenate(parts, axis=0)
        slots = jnp.dot(sel[...], rows, preferred_element_type=F32).astype(BF16)
        sent[k] = slots.reshape(PAIRS, 16, BW)
        landed[k, 0] = slots[0:16]
        for dz, dy, dx in AWAY:
            n = dz * 16 + dy * 4 + dx
            to(sent.at[k, n], landed.at[k, n], slot_send.at[k], slot_recv.at[k],
               dz=dz, dy=dy, dx=dx).start()

    def out_copy(chunk):
        return pltpu.make_async_copy(
            out.at[chunk],
            out_hbm.at[:, pl.ds(pl.multiple_of(chunk * 2 * BW, 2 * BW), 2 * BW)],
            out_sem.at[chunk],
        )

    def touch_down(k):
        whole(landed.at[k, pl.ds(1, PAIRS - 1)], slot_recv.at[k])
        total = jnp.dot(
            land[...], landed[k].reshape(16 * PAIRS, BW), preferred_element_type=F32
        )
        for part in range(2):
            out[k, :, part * BW : part * BW + BW] = total[part * HR : part * HR + HR]
        out_copy(k).start()

    def step(i, _):
        @pl.when(i < NC)
        def _():
            slab = lax.rem(i, 4)
            columns = pl.ds(pl.multiple_of(i * CW, CW), CW)
            def product(first, number):
                block = jnp.dot(
                    coef_t[first : first + number].reshape(number * HB, NQ), q[:, columns],
                    preferred_element_type=F32,
                ) * SCALE
                return block.reshape(number, HB, CW)

            block = product(10, 6)
            for k, slot in enumerate(Z2X + ZPX + ZMX[::-1]):
                put(i, k, block[slot - 10])
            for m in (0, 1, 2, 10, 11):
                message(m, i).start()
            block = product(0, 10)
            for slot, k in KEEP.items():
                prod[slab, k] = block[slot]
            put(i, 6, block[ZP])
            put(i, 7, block[ZM + 1])
            for m in (3, 4):
                message(m, i).start()

        @pl.when((i >= 1) & (i <= NC))
        def _():
            k = i - 1
            message(0, k).wait_recv()
            put(k, 9, kept(k, Z2) + got(k, 0))
            message(6, k).start()
            put(k, 8, kept(k, Z2 + 1) + got(k, 1))
            message(5, k).start()
            for m in (1, 2, 10, 11):
                message(m, k).wait_recv()
            put(k, 10, kept(k, XN) + got(k, 2) + by_z(k, 5))
            put(k, 11, kept(k, XN + 1) + by_z(k, 3) + got(k, 4))
            message(7, k).start()

        @pl.when((i >= 2) & (i <= NC + 1))
        def _():
            k = i - 2
            message(5, k).wait_recv()
            put(k, 12, kept(k, ZP + 1) + got(k, 8) + by_x(k, 3))
            message(8, k).start()
            message(6, k).wait_recv()
            put(k, 13, kept(k, ZM) + got(k, 9) + by_x(k, 5))
            message(9, k).start()

        @pl.when((i >= 3) & (i <= NC + 2))
        def _():
            k = i - 3
            for m in (3, 4, 7, 8, 9):
                message(m, k).wait_recv()
            low = kept(k, SELF) + got(k, 6) + got(k, 13) + got(k, 10)
            high = kept(k, SELF + 1) + got(k, 7) + got(k, 12) + got(k, 11)
            grad[k, 0, 0:HB] = low.astype(BF16)
            grad[k, 0, HB:CB] = high.astype(BF16)
            core_copy(k).start()

        @pl.when((i >= 3 + PER) & (lax.rem(i - 3, PER) == 0))
        def _():
            dispatch(lax.div(i - 3, PER) - 1)

        @pl.when(i == NC - 1)
        def _():
            for k in range(4):
                coef[pl.ds(k * 256, 256), :] = jnp.transpose(
                    coef_t[:, :, k * 256 : k * 256 + 256].reshape(16 * HB, 256)
                )

        @pl.when(i >= NC - 1)
        def _():
            query_part(i - (NC - 1))

        return 0

    def query_part(k):
        @pl.when(k >= 2)
        def _():
            qg_copy(k - 2).wait()

        for half in range(QW // 256):
            columns = pl.ds(pl.multiple_of(k * QW + half * 256, 256), 256)
            total = jnp.dot(
                coef[...], c[:, :, columns].reshape(16 * HB, 256), preferred_element_type=F32
            )
            qg[lax.rem(k, 2), :, half * 256 : half * 256 + 256] = (total * SCALE).astype(BF16)
        qg_copy(k).start()

    lax.fori_loop(0, NC + 4, step, 0)

    def land_part(k, _):
        touch_down(k)
        return 0

    lax.fori_loop(0, ND, land_part, 0)

    for copy in gather.values():
        copy.wait_send()

    for copy in tell_core + tell_x + tell_y + tell_z:
        copy.wait_send()

    def drain(i, _):
        for m in range(NM):
            message(m, i).wait_send()
        core_copy(i).wait_send()
        return 0

    lax.fori_loop(0, NC, drain, 0)
    for k in range(ND):
        whole(sent.at[k, pl.ds(1, PAIRS - 1)], slot_send.at[k])
        out_copy(k).wait()
    qg_copy(D // QW - 2).wait()
    qg_copy(D // QW - 1).wait()


def per_device(queries, candidates, loss_weight, positives, producers, rows):
    vmem, hbm = pl.BlockSpec(memory_space=pltpu.VMEM), pl.BlockSpec(memory_space=pl.ANY)
    shard_row = producers.reshape(1, CB)
    return pl.pallas_call(
        main_kernel,
        out_shape=(
            jax.ShapeDtypeStruct((1, NQ, D), BF16),
            jax.ShapeDtypeStruct((HR, D), F32),
        ),
        in_specs=[hbm, hbm, vmem, vmem, vmem, vmem],
        out_specs=(hbm, hbm),
        scratch_shapes=[
            pltpu.VMEM((NQ, D), BF16),
            pltpu.VMEM((16, HB, D), BF16),
            pltpu.VMEM((16, HB, NQ), F32),
            pltpu.VMEM((16, HB, NQ), BF16),
            pltpu.VMEM((NQ, 16 * HB), BF16),
            pltpu.VMEM((4, len(KEEP), HB, CW), F32),
            pltpu.VMEM((NC, 14 * HB, CW), BF16),
            pltpu.VMEM((NC, 14 * HB, CW), BF16),
            pltpu.VMEM((2, NQ, QW), BF16),
            pltpu.VMEM((16 * PAIRS, 4 * CB), BF16),
            pltpu.VMEM((8, NQ), F32),
            pltpu.VMEM((8, NQ), F32),
            pltpu.VMEM((4, 4, 4, 2, 2, CB), I32),
            pltpu.VMEM((2 * HR, 8 * SHARDS), BF16),
            pltpu.VMEM((ND, HR, 2 * BW), F32),
            pltpu.VMEM((NC, 2, CB, CW), BF16),
            pltpu.VMEM((ND, PAIRS, 16, BW), BF16),
            pltpu.VMEM((ND, PAIRS, 16, BW), BF16),
            pltpu.SemaphoreType.DMA,
            pltpu.SemaphoreType.DMA((2,)),
            pltpu.SemaphoreType.DMA((18,)),
            pltpu.SemaphoreType.DMA((18,)),
            pltpu.SemaphoreType.DMA((NC, NM)),
            pltpu.SemaphoreType.DMA((NC, NM)),
            pltpu.SemaphoreType.DMA((2,)),
            pltpu.SemaphoreType.DMA((ND,)),
            pltpu.SemaphoreType.DMA((10,)),
            pltpu.SemaphoreType.DMA((10,)),
            pltpu.SemaphoreType.DMA((NC,)),
            pltpu.SemaphoreType.DMA((NC,)),
            pltpu.SemaphoreType.DMA((ND,)),
            pltpu.SemaphoreType.DMA((ND,)),
        ],
        compiler_params=pltpu.CompilerParams(
            collective_id=0, has_side_effects=True, vmem_limit_bytes=62 * 2**20
        ),
        cost_estimate=pl.CostEstimate(
            flops=6 * NQ * NQ * D, bytes_accessed=20 * 2**20, transcendentals=NQ * NQ
        ),
        name="listwise_backward",
    )(queries, candidates, loss_weight, positives, shard_row, rows)


def solution(mesh):
    return jax.shard_map(
        per_device,
        mesh=mesh,
        in_specs=(
            P("dp", "blk", None),
            P("dp", "blk", None),
            P("dp", "blk"),
            P("dp", "blk"),
            P("dp", "blk", None),
            P("dp", "blk"),
        ),
        out_specs=(P("dp", "blk", None), P(("blk", "dp"), None)),
        check_vma=False,
    )
```

```python
import functools
import math

import jax
import jax.numpy as jnp
from jax import lax
from jax.experimental import pallas as pl
from jax.experimental.pallas import tpu as pltpu
from jax.sharding import PartitionSpec as P

D = 2560
HR = 256
MOST = 4
NQ = 1024
CB = 128
HB = 64
STAY = 32
NC = 5
CW = D // NC
ND = 5
PER = NC // ND
QW = 512
BW = D // ND // 2
SHARDS = 128
SCALE = 1.0 / math.sqrt(D)
F32, BF16, I32 = jnp.float32, jnp.bfloat16, jnp.int32

SELF, XN, ZP, ZM, Z2 = 0, 2, 4, 6, 8
ZPX, ZMX, Z2X = (10, 13), (11, 14), (12, 15)
GROUPS = ((0, 4), (4, 4), (8, 5), (13, 3))

MESSAGES = (
    (0, 128, "x"), (128, 64 + STAY, "p"), (256, 64 + STAY, "m"), (384, 64, "p"), (448, 64, "m"),
    (512, 64, "p"), (576, 64, "m"), (640, 128, "x"), (768, 64, "p"), (832, 64, "m"),
    (192 + STAY, 64 - STAY, "x"), (320 + STAY, 64 - STAY, "x"),
)
NM = len(MESSAGES)
KEEP = {SELF: 0, SELF + 1: 1, XN: 2, XN + 1: 3, ZP: 4, ZP + 1: 5, ZM: 6, ZM + 1: 7, Z2: 8, Z2 + 1: 9}
PAIRS = SHARDS // 2

AWAY = sorted(
    ((n // 16, n // 4 % 4, n % 4) for n in range(1, PAIRS)),
    key=lambda way: -sum(min(far, 4 - far) for far in way),
)


def main_kernel(
    q_hbm, c_hbm, w_ref, pos_ref, shard_ref, row_ref, qg_hbm, out_hbm,
    q, c, e, coef_t, coef, prod, snd, rcv, qg, sel, mx, sm, meta, land, out,
    grad, sent, landed,
    q_sem, c_sem, ag_send, ag_recv, rs_send, rs_recv, qg_sem, out_sem,
    meta_send, meta_recv, core_send, core_recv, slot_send, slot_recv,
):
    blk, dp = lax.axis_index("blk"), lax.axis_index("dp")
    z, x_lo = lax.div(blk, 2), lax.rem(blk, 2)
    x_hi, y, core = lax.div(dp, 8), lax.rem(lax.div(dp, 2), 4), lax.rem(dp, 2)
    x = x_hi * 2 + x_lo

    def at(dz, dx):
        return lax.rem(z + dz, 4) * 2 + lax.rem(x_lo + dx, 2)

    def device(dz=0, dy=0, dx=0, dc=0):
        across = lax.rem(x + dx, 4)
        return {
            "blk": lax.rem(z + dz, 4) * 2 + lax.rem(across, 2),
            "dp": lax.div(across, 2) * 8 + lax.rem(y + dy, 4) * 2 + lax.rem(core + dc, 2),
        }

    def to(src, dst, send, recv, **way):
        return pltpu.make_async_remote_copy(
            src_ref=src, dst_ref=dst, send_sem=send, recv_sem=recv,
            device_id=device(**way), device_id_type=pl.DeviceIdType.MESH,
        )

    def whole(ref, sem):
        pltpu.make_async_copy(ref, ref, sem).wait()

    peers = {"x": at(0, 1), "p": at(1, 0), "m": at(3, 0)}

    q_copy = pltpu.make_async_copy(q_hbm.at[0], q, q_sem)
    q_copy.start()
    own = [
        pltpu.make_async_copy(c_hbm.at[0, pl.ds(h * HB, HB)], c.at[h], c_sem.at[h]) for h in (0, 1)
    ]
    for copy in own:
        copy.start()

    meta[0, 0, 0, 0, 0:1, :] = shard_ref[...]
    meta[0, 0, 0, 0, 1:2, :] = row_ref[...]
    lines = [{"dc": 1}] + [{"dz": dz, "dy": dy, "dx": dx} for dz, dy, dx in AWAY]
    barrier = pltpu.get_barrier_semaphore()
    for line in lines:
        pl.semaphore_signal(
            barrier, inc=1, device_id=device(**line), device_id_type=pl.DeviceIdType.MESH
        )
    pl.semaphore_wait(barrier, len(lines))

    def ag(src, dst, way, first=0, number=HB, sem=None):
        if src < 2:
            source = c_hbm.at[0, pl.ds(src * HB + first, number)]
        else:
            source = c.at[src, pl.ds(first, number)]
        sem = dst if sem is None else sem
        return pltpu.make_async_remote_copy(
            src_ref=source,
            dst_ref=c.at[dst, pl.ds(first, number)],
            send_sem=ag_send.at[sem],
            recv_sem=ag_recv.at[sem],
            device_id={"blk": peers[way]},
            device_id_type=pl.DeviceIdType.MESH,
        )

    gather = {
        ZM: ag(0, ZM, "p"), ZP + 1: ag(1, ZP + 1, "m"), XN: ag(0, XN, "x"),
        ZM + 1: ag(1, ZM + 1, "p"), ZP: ag(0, ZP, "m"), XN + 1: ag(1, XN + 1, "x"),
        Z2: ag(ZM, Z2, "p"), Z2 + 1: ag(ZP + 1, Z2 + 1, "m"),
        ZMX[0]: ag(XN, ZMX[0], "p"), ZPX[0]: ag(XN, ZPX[0], "m"),
        ZMX[1]: ag(XN + 1, ZMX[1], "p", 0, STAY), ZPX[1]: ag(XN + 1, ZPX[1], "m", 0, STAY),
        16: ag(ZM + 1, ZMX[1], "x", STAY, HB - STAY, 16),
        17: ag(ZP + 1, ZPX[1], "x", STAY, HB - STAY, 17),
        Z2X[0]: ag(Z2, Z2X[0], "x"), Z2X[1]: ag(Z2 + 1, Z2X[1], "x"),
    }
    for slot in (ZM, ZP + 1, XN, ZM + 1, ZP, XN + 1):
        gather[slot].start()

    def tell(k, src, dst, **way):
        return to(src, dst, meta_send.at[k], meta_recv.at[k], **way)

    tell_core = [tell(0, meta.at[0, 0, 0, 0], meta.at[0, 0, 0, 1], dc=1)]
    tell_x = [tell(far, meta.at[0, 0, 0], meta.at[0, 0, far], dx=far) for far in (1, 2, 3)]
    tell_y = [tell(3 + far, meta.at[0, 0], meta.at[0, far], dy=far) for far in (1, 2, 3)]
    tell_z = [tell(6 + far, meta.at[0], meta.at[far], dz=far) for far in (1, 2, 3)]
    for copy in tell_core:
        copy.start()

    for copy in tell_core:
        copy.wait_recv()
    for copy in tell_x:
        copy.start()

    keys = []
    for chip_core in range(2):
        shard = meta[0, 0, 0, chip_core, 0:1, :]
        wide = jnp.broadcast_to(shard, (CB, CB))
        earlier = (jnp.transpose(wide) == wide) & (
            lax.broadcasted_iota(I32, (CB, CB), 0) < lax.broadcasted_iota(I32, (CB, CB), 1)
        )
        place = jnp.sum(earlier.astype(I32), axis=0, keepdims=True)
        keys.append((shard * MOST + place) * 4 + chip_core * 2)
    keys = jnp.concatenate([keys[0], keys[1], keys[0] + 1, keys[1] + 1], axis=1)

    def fill(i, _):
        row = i * 256 + lax.broadcasted_iota(I32, (256, 1), 0)
        block = row // 16
        across = (x + block % 4) % 4
        to_shard = ((z + block // 16) % 4 * 2 + across % 2) * 16 + (
            across // 2 * 8 + (y + block // 4 % 4) % 4 * 2 + core
        )
        key = (to_shard * MOST + row % 4) * 4 + row // 4 % 4
        sel[pl.ds(pl.multiple_of(i * 256, 256), 256), :] = (key == keys).astype(F32).astype(BF16)
        return 0

    lax.fori_loop(0, 16 * PAIRS // 256, fill, 0)
    q_copy.wait()
    for copy in own:
        copy.wait()

    def scores(which):
        first, number = GROUPS[which]

        def part(i, _):
            span = pl.ds(pl.multiple_of(i * 256, 256), 256)
            s = lax.dot_general(
                c[first : first + number].reshape(number * HB, D), q[span, :],
                (((1,), (1,)), ((), ())), preferred_element_type=F32,
            ) * SCALE
            top = jnp.max(s, axis=0, keepdims=True)
            shifted = jnp.exp(s - top)
            e[first : first + number, :, span] = shifted.reshape(number, HB, 256)
            mx[which : which + 1, span] = top
            sm[which : which + 1, span] = jnp.sum(shifted, axis=0, keepdims=True)
            return 0

        lax.fori_loop(0, NQ // 256, part, 0)

    def landing_rows():
        for copy in tell_z:
            copy.wait_recv()
        everyone = meta[...].reshape(SHARDS, 2, CB)
        shards, numbers = everyone[:, 0, :], everyone[:, 1, :]
        hits = (shards == blk * 16 + dp).astype(F32)
        before = (
            lax.broadcasted_iota(I32, (CB, CB), 0) < lax.broadcasted_iota(I32, (CB, CB), 1)
        ).astype(F32).astype(BF16)
        spot = jnp.dot(hits.astype(BF16), before, preferred_element_type=F32)
        numbers = (numbers + 1).astype(F32) * hits
        lanes = lax.broadcasted_iota(I32, (SHARDS, 8 * SHARDS), 1)
        spread = lanes // 8 == lax.broadcasted_iota(I32, (SHARDS, 8 * SHARDS), 0)
        spread = spread.astype(F32).astype(BF16)
        slot = lax.broadcasted_iota(I32, (8, 8 * SHARDS), 1) % 4
        key = jnp.zeros((8, 8 * SHARDS), F32)
        for k in range(MOST):
            chosen = jnp.where(spot == float(k), numbers, 0.0).astype(BF16)
            by_source = lax.dot_general(
                jnp.ones((8, CB), BF16), chosen, (((1,), (1,)), ((), ())),
                preferred_element_type=F32,
            )
            by_slot = jnp.dot(by_source.astype(BF16), spread, preferred_element_type=F32)
            key = key + jnp.where(slot == k, by_slot, 0.0)
        key = key[0:1].astype(I32) - 1
        part = lax.broadcasted_iota(I32, (1, 8 * SHARDS), 1) // 4 % 2
        for k in range(2):
            mine = jnp.where(part == k, key, -1)
            for piece in range(HR // 64):
                rows = piece * 64 + lax.broadcasted_iota(I32, (64, 8 * SHARDS), 0)
                first = k * HR + piece * 64
                land[first : first + 64, :] = (rows == mine).astype(F32).astype(BF16)

    gather[ZM].wait_recv()
    gather[Z2].start()
    gather[ZP + 1].wait_recv()
    gather[Z2 + 1].start()
    gather[XN].wait_recv()
    gather[XN + 1].wait_recv()
    scores(0)
    for copy in tell_x:
        copy.wait_recv()
    for copy in tell_y:
        copy.start()
    gather[17].start()
    gather[ZM + 1].wait_recv()
    gather[16].start()
    gather[ZP].wait_recv()
    scores(1)
    for copy in tell_y:
        copy.wait_recv()
    for copy in tell_z:
        copy.start()
    gather[Z2].wait_recv()
    gather[Z2X[0]].start()
    gather[Z2 + 1].wait_recv()
    gather[Z2X[1]].start()
    for slot in (ZMX[0], ZPX[0], ZMX[1], ZPX[1]):
        gather[slot].start()
    landing_rows()
    for slot in (ZPX[0], ZMX[0], Z2X[0]):
        gather[slot].wait_recv()
    scores(2)
    for slot in (ZPX[1], ZMX[1], 16, 17, Z2X[1]):
        gather[slot].wait_recv()
    scores(3)

    top = jnp.max(mx[0:4], axis=0, keepdims=True)
    rescale = jnp.exp(mx[0:4] - top)
    inverse = 1.0 / jnp.sum(rescale * sm[0:4], axis=0, keepdims=True)
    weight, target = w_ref[...], pos_ref[...]
    places = {
        0: at(0, 0), 2: at(0, 1), 4: at(1, 0), 6: at(3, 0), 8: at(2, 0),
    }
    starts = [0] * 16
    for first, owner in places.items():
        starts[first], starts[first + 1] = owner * CB, owner * CB + HB
    for (low, high), owner in ((ZPX, at(1, 1)), (ZMX, at(3, 1)), (Z2X, at(2, 1))):
        starts[low], starts[high] = owner * CB, owner * CB + HB
    for which, (first, number) in enumerate(GROUPS):
        factor = rescale[which : which + 1] * inverse
        for k in range(first, first + number):
            ids = starts[k] + lax.broadcasted_iota(I32, (HB, NQ), 0)
            onehot = (ids == target).astype(F32)
            coef_t[k] = (weight * (e[k] * factor - onehot)).astype(BF16)

    def message(m, chunk):
        first, number, way = MESSAGES[m]
        return pltpu.make_async_remote_copy(
            src_ref=snd.at[chunk, pl.ds(first, number)],
            dst_ref=rcv.at[chunk, pl.ds(first, number)],
            send_sem=rs_send.at[chunk, m],
            recv_sem=rs_recv.at[chunk, m],
            device_id={"blk": peers[way]},
            device_id_type=pl.DeviceIdType.MESH,
        )

    def qg_copy(chunk):
        return pltpu.make_async_copy(
            qg.at[lax.rem(chunk, 2)],
            qg_hbm.at[0, :, pl.ds(pl.multiple_of(chunk * QW, QW), QW)],
            qg_sem.at[lax.rem(chunk, 2)],
        )

    def put(chunk, slot, value):
        snd[chunk, slot * HB : slot * HB + HB] = value.astype(BF16)

    def got(chunk, slot):
        return rcv[chunk, slot * HB : slot * HB + HB].astype(F32)

    def by_z(chunk, slot):
        return jnp.where(lax.broadcasted_iota(I32, (HB, CW), 0) < STAY, got(chunk, slot), 0.0)

    def by_x(chunk, slot):
        return jnp.where(lax.broadcasted_iota(I32, (HB, CW), 0) >= STAY, got(chunk, slot), 0.0)

    def kept(chunk, slot):
        return prod[lax.rem(chunk, 4), KEEP[slot]]

    def core_copy(k):
        return to(grad.at[k, 0], grad.at[k, 1], core_send.at[k], core_recv.at[k], dc=1)

    def dispatch(k):
        parts = []
        for chunk in range(PER):
            core_copy(k * PER + chunk).wait_recv()
        for part in range(2):
            for chip_core in range(2):
                first = part * BW
                while first < part * BW + BW:
                    width = min(BW, CW - first % CW)
                    parts.append(grad[k * PER + first // CW, chip_core, :, first % CW : first % CW + width])
                    first += width
        assert len(parts) == 4
        rows = jnp.concatenate(parts, axis=0)
        slots = jnp.dot(sel[...], rows, preferred_element_type=F32).astype(BF16)
        sent[k] = slots.reshape(PAIRS, 16, BW)
        landed[k, 0] = slots[0:16]
        for dz, dy, dx in AWAY:
            n = dz * 16 + dy * 4 + dx
            to(sent.at[k, n], landed.at[k, n], slot_send.at[k], slot_recv.at[k],
               dz=dz, dy=dy, dx=dx).start()

    def out_copy(chunk):
        return pltpu.make_async_copy(
            out.at[chunk],
            out_hbm.at[:, pl.ds(pl.multiple_of(chunk * 2 * BW, 2 * BW), 2 * BW)],
            out_sem.at[chunk],
        )

    def touch_down(k):
        whole(landed.at[k, pl.ds(1, PAIRS - 1)], slot_recv.at[k])
        total = jnp.dot(
            land[...], landed[k].reshape(16 * PAIRS, BW), preferred_element_type=F32
        )
        for part in range(2):
            out[k, :, part * BW : part * BW + BW] = total[part * HR : part * HR + HR]
        out_copy(k).start()

    def step(i, _):
        @pl.when(i < NC)
        def _():
            slab = lax.rem(i, 4)
            columns = pl.ds(pl.multiple_of(i * CW, CW), CW)
            def product(first, number):
                block = jnp.dot(
                    coef_t[first : first + number].reshape(number * HB, NQ), q[:, columns],
                    preferred_element_type=F32,
                ) * SCALE
                return block.reshape(number, HB, CW)

            block = product(10, 6)
            for k, slot in enumerate(Z2X + ZPX + ZMX[::-1]):
                put(i, k, block[slot - 10])
            for m in (0, 1, 2, 10, 11):
                message(m, i).start()
            block = product(0, 10)
            for slot, k in KEEP.items():
                prod[slab, k] = block[slot]
            put(i, 6, block[ZP])
            put(i, 7, block[ZM + 1])
            for m in (3, 4):
                message(m, i).start()

        @pl.when((i >= 1) & (i <= NC))
        def _():
            k = i - 1
            message(0, k).wait_recv()
            put(k, 9, kept(k, Z2) + got(k, 0))
            message(6, k).start()
            put(k, 8, kept(k, Z2 + 1) + got(k, 1))
            message(5, k).start()
            for m in (1, 2, 10, 11):
                message(m, k).wait_recv()
            put(k, 10, kept(k, XN) + got(k, 2) + by_z(k, 5))
            put(k, 11, kept(k, XN + 1) + by_z(k, 3) + got(k, 4))
            message(7, k).start()

        @pl.when((i >= 2) & (i <= NC + 1))
        def _():
            k = i - 2
            message(5, k).wait_recv()
            put(k, 12, kept(k, ZP + 1) + got(k, 8) + by_x(k, 3))
            message(8, k).start()
            message(6, k).wait_recv()
            put(k, 13, kept(k, ZM) + got(k, 9) + by_x(k, 5))
            message(9, k).start()

        @pl.when((i >= 3) & (i <= NC + 2))
        def _():
            k = i - 3
            for m in (3, 4, 7, 8, 9):
                message(m, k).wait_recv()
            low = kept(k, SELF) + got(k, 6) + got(k, 13) + got(k, 10)
            high = kept(k, SELF + 1) + got(k, 7) + got(k, 12) + got(k, 11)
            grad[k, 0, 0:HB] = low.astype(BF16)
            grad[k, 0, HB:CB] = high.astype(BF16)
            core_copy(k).start()

        @pl.when((i >= 3 + PER) & (lax.rem(i - 3, PER) == 0))
        def _():
            dispatch(lax.div(i - 3, PER) - 1)

        @pl.when(i == NC - 1)
        def _():
            for k in range(4):
                coef[pl.ds(k * 256, 256), :] = jnp.transpose(
                    coef_t[:, :, k * 256 : k * 256 + 256].reshape(16 * HB, 256)
                )

        @pl.when(i >= NC - 1)
        def _():
            query_part(i - (NC - 1))

        return 0

    def query_part(k):
        @pl.when(k >= 2)
        def _():
            qg_copy(k - 2).wait()

        for half in range(QW // 256):
            columns = pl.ds(pl.multiple_of(k * QW + half * 256, 256), 256)
            total = jnp.dot(
                coef[...], c[:, :, columns].reshape(16 * HB, 256), preferred_element_type=F32
            )
            qg[lax.rem(k, 2), :, half * 256 : half * 256 + 256] = (total * SCALE).astype(BF16)
        qg_copy(k).start()

    lax.fori_loop(0, NC + 4, step, 0)

    def land_part(k, _):
        touch_down(k)
        return 0

    lax.fori_loop(0, ND, land_part, 0)

    for copy in gather.values():
        copy.wait_send()

    for copy in tell_core + tell_x + tell_y + tell_z:
        copy.wait_send()

    def drain(i, _):
        for m in range(NM):
            message(m, i).wait_send()
        core_copy(i).wait_send()
        return 0

    lax.fori_loop(0, NC, drain, 0)
    for k in range(ND):
        whole(sent.at[k, pl.ds(1, PAIRS - 1)], slot_send.at[k])
        out_copy(k).wait()
    qg_copy(D // QW - 2).wait()
    qg_copy(D // QW - 1).wait()


def per_device(queries, candidates, loss_weight, positives, producers, rows):
    vmem, hbm = pl.BlockSpec(memory_space=pltpu.VMEM), pl.BlockSpec(memory_space=pl.ANY)
    shard_row = producers.reshape(1, CB)
    return pl.pallas_call(
        main_kernel,
        out_shape=(
            jax.ShapeDtypeStruct((1, NQ, D), BF16),
            jax.ShapeDtypeStruct((HR, D), F32),
        ),
        in_specs=[hbm, hbm, vmem, vmem, vmem, vmem],
        out_specs=(hbm, hbm),
        scratch_shapes=[
            pltpu.VMEM((NQ, D), BF16),
            pltpu.VMEM((16, HB, D), BF16),
            pltpu.VMEM((16, HB, NQ), F32),
            pltpu.VMEM((16, HB, NQ), BF16),
            pltpu.VMEM((NQ, 16 * HB), BF16),
            pltpu.VMEM((4, len(KEEP), HB, CW), F32),
            pltpu.VMEM((NC, 14 * HB, CW), BF16),
            pltpu.VMEM((NC, 14 * HB, CW), BF16),
            pltpu.VMEM((2, NQ, QW), BF16),
            pltpu.VMEM((16 * PAIRS, 4 * CB), BF16),
            pltpu.VMEM((8, NQ), F32),
            pltpu.VMEM((8, NQ), F32),
            pltpu.VMEM((4, 4, 4, 2, 2, CB), I32),
            pltpu.VMEM((2 * HR, 8 * SHARDS), BF16),
            pltpu.VMEM((ND, HR, 2 * BW), F32),
            pltpu.VMEM((NC, 2, CB, CW), BF16),
            pltpu.VMEM((ND, PAIRS, 16, BW), BF16),
            pltpu.VMEM((ND, PAIRS, 16, BW), BF16),
            pltpu.SemaphoreType.DMA,
            pltpu.SemaphoreType.DMA((2,)),
            pltpu.SemaphoreType.DMA((18,)),
            pltpu.SemaphoreType.DMA((18,)),
            pltpu.SemaphoreType.DMA((NC, NM)),
            pltpu.SemaphoreType.DMA((NC, NM)),
            pltpu.SemaphoreType.DMA((2,)),
            pltpu.SemaphoreType.DMA((ND,)),
            pltpu.SemaphoreType.DMA((10,)),
            pltpu.SemaphoreType.DMA((10,)),
            pltpu.SemaphoreType.DMA((NC,)),
            pltpu.SemaphoreType.DMA((NC,)),
            pltpu.SemaphoreType.DMA((ND,)),
            pltpu.SemaphoreType.DMA((ND,)),
        ],
        compiler_params=pltpu.CompilerParams(
            collective_id=0, has_side_effects=True, vmem_limit_bytes=62 * 2**20
        ),
        cost_estimate=pl.CostEstimate(
            flops=6 * NQ * NQ * D, bytes_accessed=20 * 2**20, transcendentals=NQ * NQ
        ),
        name="listwise_backward",
    )(queries, candidates, loss_weight, positives, shard_row, rows)


def solution(mesh):
    return jax.shard_map(
        per_device,
        mesh=mesh,
        in_specs=(
            P("dp", "blk", None),
            P("dp", "blk", None),
            P("dp", "blk"),
            P("dp", "blk"),
            P("dp", "blk", None),
            P("dp", "blk"),
        ),
        out_specs=(P("dp", "blk", None), P(("blk", "dp"), None)),
        check_vma=False,
    )
```

```python
import functools
import math

import jax
import jax.numpy as jnp
from jax import lax
from jax.experimental import pallas as pl
from jax.experimental.pallas import tpu as pltpu
from jax.sharding import PartitionSpec as P

D = 2560
HR = 256
MOST = 4
NQ = 1024
CB = 128
HB = 64
KEEP_G = 48
STAY = 32
NC = 5
CW = D // NC
ND = 5
PER = NC // ND
QW = 512
BW = D // ND // 2
SHARDS = 128
SCALE = 1.0 / math.sqrt(D)
F32, BF16, I32 = jnp.float32, jnp.bfloat16, jnp.int32

SELF, XN, ZP, ZM, Z2 = 0, 2, 4, 6, 8
ZPX, ZMX, Z2X = (10, 13), (11, 14), (12, 15)
GROUPS = ((0, 4), (4, 4), (8, 5), (13, 3))

MESSAGES = (
    (0, 128, "x"), (128, 64 + STAY, "p"), (256, 64 + STAY, "m"), (384, 64, "p"), (448, 64, "m"),
    (512, 64, "p"), (576, 64, "m"), (640, 128, "x"), (768, 64, "p"), (832, 64, "m"),
    (192 + STAY, 64 - STAY, "x"), (320 + STAY, 64 - STAY, "x"),
)
NM = len(MESSAGES)
KEEP = {SELF: 0, SELF + 1: 1, XN: 2, XN + 1: 3, ZP: 4, ZP + 1: 5, ZM: 6, ZM + 1: 7, Z2: 8, Z2 + 1: 9}
PAIRS = SHARDS // 2

AWAY = sorted(
    ((n // 16, n // 4 % 4, n % 4) for n in range(1, PAIRS)),
    key=lambda way: -sum(min(far, 4 - far) for far in way),
)


def main_kernel(
    q_hbm, c_hbm, w_ref, pos_ref, shard_ref, row_ref, qg_hbm, out_hbm,
    q, c, e, coef_t, coef, prod, snd, rcv, qg, sel, mx, sm, meta, land, out,
    grad, sent, landed,
    q_sem, c_sem, ag_send, ag_recv, rs_send, rs_recv, qg_sem, out_sem,
    meta_send, meta_recv, core_send, core_recv, slot_send, slot_recv,
):
    blk, dp = lax.axis_index("blk"), lax.axis_index("dp")
    z, x_lo = lax.div(blk, 2), lax.rem(blk, 2)
    x_hi, y, core = lax.div(dp, 8), lax.rem(lax.div(dp, 2), 4), lax.rem(dp, 2)
    x = x_hi * 2 + x_lo

    def at(dz, dx):
        return lax.rem(z + dz, 4) * 2 + lax.rem(x_lo + dx, 2)

    def device(dz=0, dy=0, dx=0, dc=0):
        across = lax.rem(x + dx, 4)
        return {
            "blk": lax.rem(z + dz, 4) * 2 + lax.rem(across, 2),
            "dp": lax.div(across, 2) * 8 + lax.rem(y + dy, 4) * 2 + lax.rem(core + dc, 2),
        }

    def to(src, dst, send, recv, **way):
        return pltpu.make_async_remote_copy(
            src_ref=src, dst_ref=dst, send_sem=send, recv_sem=recv,
            device_id=device(**way), device_id_type=pl.DeviceIdType.MESH,
        )

    def whole(ref, sem):
        pltpu.make_async_copy(ref, ref, sem).wait()

    peers = {"x": at(0, 1), "p": at(1, 0), "m": at(3, 0)}

    q_copy = pltpu.make_async_copy(q_hbm.at[0], q, q_sem)
    q_copy.start()
    own = [
        pltpu.make_async_copy(c_hbm.at[0, pl.ds(h * HB, HB)], c.at[h], c_sem.at[h]) for h in (0, 1)
    ]
    for copy in own:
        copy.start()

    meta[0, 0, 0, 0, 0:1, :] = shard_ref[...]
    meta[0, 0, 0, 0, 1:2, :] = row_ref[...]
    lines = [{"dc": 1}] + [{"dz": dz, "dy": dy, "dx": dx} for dz, dy, dx in AWAY]
    barrier = pltpu.get_barrier_semaphore()
    for line in lines:
        pl.semaphore_signal(
            barrier, inc=1, device_id=device(**line), device_id_type=pl.DeviceIdType.MESH
        )
    pl.semaphore_wait(barrier, len(lines))

    def ag(src, dst, way, first=0, number=HB, sem=None):
        if src < 2:
            source = c_hbm.at[0, pl.ds(src * HB + first, number)]
        else:
            source = c.at[src, pl.ds(first, number)]
        sem = dst if sem is None else sem
        return pltpu.make_async_remote_copy(
            src_ref=source,
            dst_ref=c.at[dst, pl.ds(first, number)],
            send_sem=ag_send.at[sem],
            recv_sem=ag_recv.at[sem],
            device_id={"blk": peers[way]},
            device_id_type=pl.DeviceIdType.MESH,
        )

    gather = {
        ZM: ag(0, ZM, "p"), ZP + 1: ag(1, ZP + 1, "m"), XN: ag(0, XN, "x"),
        ZM + 1: ag(1, ZM + 1, "p"), ZP: ag(0, ZP, "m"), XN + 1: ag(1, XN + 1, "x"),
        Z2: ag(ZM, Z2, "p"), Z2 + 1: ag(ZP + 1, Z2 + 1, "m"),
        ZMX[0]: ag(XN, ZMX[0], "p"), ZPX[0]: ag(XN, ZPX[0], "m"),
        ZMX[1]: ag(XN + 1, ZMX[1], "p", 0, KEEP_G), ZPX[1]: ag(XN + 1, ZPX[1], "m", 0, KEEP_G),
        16: ag(ZM + 1, ZMX[1], "x", KEEP_G, HB - KEEP_G, 16),
        17: ag(ZP + 1, ZPX[1], "x", KEEP_G, HB - KEEP_G, 17),
        Z2X[0]: ag(Z2, Z2X[0], "x"), Z2X[1]: ag(Z2 + 1, Z2X[1], "x"),
    }
    for slot in (ZM, ZP + 1, XN, ZM + 1, ZP, XN + 1):
        gather[slot].start()

    def tell(k, src, dst, **way):
        return to(src, dst, meta_send.at[k], meta_recv.at[k], **way)

    tell_core = [tell(0, meta.at[0, 0, 0, 0], meta.at[0, 0, 0, 1], dc=1)]
    tell_x = [tell(far, meta.at[0, 0, 0], meta.at[0, 0, far], dx=far) for far in (1, 2, 3)]
    tell_y = [tell(3 + far, meta.at[0, 0], meta.at[0, far], dy=far) for far in (1, 2, 3)]
    tell_z = [tell(6 + far, meta.at[0], meta.at[far], dz=far) for far in (1, 2, 3)]
    for copy in tell_core:
        copy.start()

    for copy in tell_core:
        copy.wait_recv()
    for copy in tell_x:
        copy.start()

    keys = []
    for chip_core in range(2):
        shard = meta[0, 0, 0, chip_core, 0:1, :]
        wide = jnp.broadcast_to(shard, (CB, CB))
        earlier = (jnp.transpose(wide) == wide) & (
            lax.broadcasted_iota(I32, (CB, CB), 0) < lax.broadcasted_iota(I32, (CB, CB), 1)
        )
        place = jnp.sum(earlier.astype(I32), axis=0, keepdims=True)
        keys.append((shard * MOST + place) * 4 + chip_core * 2)
    keys = jnp.concatenate([keys[0], keys[1], keys[0] + 1, keys[1] + 1], axis=1)

    def fill(i, _):
        row = i * 256 + lax.broadcasted_iota(I32, (256, 1), 0)
        block = row // 16
        across = (x + block % 4) % 4
        to_shard = ((z + block // 16) % 4 * 2 + across % 2) * 16 + (
            across // 2 * 8 + (y + block // 4 % 4) % 4 * 2 + core
        )
        key = (to_shard * MOST + row % 4) * 4 + row // 4 % 4
        sel[pl.ds(pl.multiple_of(i * 256, 256), 256), :] = (key == keys).astype(F32).astype(BF16)
        return 0

    lax.fori_loop(0, 16 * PAIRS // 256, fill, 0)
    q_copy.wait()
    for copy in own:
        copy.wait()

    def scores(which):
        first, number = GROUPS[which]

        def part(i, _):
            span = pl.ds(pl.multiple_of(i * 256, 256), 256)
            s = lax.dot_general(
                c[first : first + number].reshape(number * HB, D), q[span, :],
                (((1,), (1,)), ((), ())), preferred_element_type=F32,
            ) * SCALE
            top = jnp.max(s, axis=0, keepdims=True)
            shifted = jnp.exp(s - top)
            e[first : first + number, :, span] = shifted.reshape(number, HB, 256)
            mx[which : which + 1, span] = top
            sm[which : which + 1, span] = jnp.sum(shifted, axis=0, keepdims=True)
            return 0

        lax.fori_loop(0, NQ // 256, part, 0)

    def landing_rows():
        for copy in tell_z:
            copy.wait_recv()
        everyone = meta[...].reshape(SHARDS, 2, CB)
        shards, numbers = everyone[:, 0, :], everyone[:, 1, :]
        hits = (shards == blk * 16 + dp).astype(F32)
        before = (
            lax.broadcasted_iota(I32, (CB, CB), 0) < lax.broadcasted_iota(I32, (CB, CB), 1)
        ).astype(F32).astype(BF16)
        spot = jnp.dot(hits.astype(BF16), before, preferred_element_type=F32)
        numbers = (numbers + 1).astype(F32) * hits
        lanes = lax.broadcasted_iota(I32, (SHARDS, 8 * SHARDS), 1)
        spread = lanes // 8 == lax.broadcasted_iota(I32, (SHARDS, 8 * SHARDS), 0)
        spread = spread.astype(F32).astype(BF16)
        slot = lax.broadcasted_iota(I32, (8, 8 * SHARDS), 1) % 4
        key = jnp.zeros((8, 8 * SHARDS), F32)
        for k in range(MOST):
            chosen = jnp.where(spot == float(k), numbers, 0.0).astype(BF16)
            by_source = lax.dot_general(
                jnp.ones((8, CB), BF16), chosen, (((1,), (1,)), ((), ())),
                preferred_element_type=F32,
            )
            by_slot = jnp.dot(by_source.astype(BF16), spread, preferred_element_type=F32)
            key = key + jnp.where(slot == k, by_slot, 0.0)
        key = key[0:1].astype(I32) - 1
        part = lax.broadcasted_iota(I32, (1, 8 * SHARDS), 1) // 4 % 2
        for k in range(2):
            mine = jnp.where(part == k, key, -1)
            for piece in range(HR // 64):
                rows = piece * 64 + lax.broadcasted_iota(I32, (64, 8 * SHARDS), 0)
                first = k * HR + piece * 64
                land[first : first + 64, :] = (rows == mine).astype(F32).astype(BF16)

    gather[ZM].wait_recv()
    gather[Z2].start()
    gather[ZP + 1].wait_recv()
    gather[Z2 + 1].start()
    gather[XN].wait_recv()
    gather[XN + 1].wait_recv()
    scores(0)
    for copy in tell_x:
        copy.wait_recv()
    for copy in tell_y:
        copy.start()
    gather[17].start()
    gather[ZM + 1].wait_recv()
    gather[16].start()
    gather[ZP].wait_recv()
    scores(1)
    for copy in tell_y:
        copy.wait_recv()
    for copy in tell_z:
        copy.start()
    gather[Z2].wait_recv()
    gather[Z2X[0]].start()
    gather[Z2 + 1].wait_recv()
    gather[Z2X[1]].start()
    for slot in (ZMX[0], ZPX[0], ZMX[1], ZPX[1]):
        gather[slot].start()
    landing_rows()
    for slot in (ZPX[0], ZMX[0], Z2X[0]):
        gather[slot].wait_recv()
    scores(2)
    for slot in (ZPX[1], ZMX[1], 16, 17, Z2X[1]):
        gather[slot].wait_recv()
    scores(3)

    top = jnp.max(mx[0:4], axis=0, keepdims=True)
    rescale = jnp.exp(mx[0:4] - top)
    inverse = 1.0 / jnp.sum(rescale * sm[0:4], axis=0, keepdims=True)
    weight, target = w_ref[...], pos_ref[...]
    places = {
        0: at(0, 0), 2: at(0, 1), 4: at(1, 0), 6: at(3, 0), 8: at(2, 0),
    }
    starts = [0] * 16
    for first, owner in places.items():
        starts[first], starts[first + 1] = owner * CB, owner * CB + HB
    for (low, high), owner in ((ZPX, at(1, 1)), (ZMX, at(3, 1)), (Z2X, at(2, 1))):
        starts[low], starts[high] = owner * CB, owner * CB + HB
    for which, (first, number) in enumerate(GROUPS):
        factor = rescale[which : which + 1] * inverse
        for k in range(first, first + number):
            ids = starts[k] + lax.broadcasted_iota(I32, (HB, NQ), 0)
            onehot = (ids == target).astype(F32)
            coef_t[k] = (weight * (e[k] * factor - onehot)).astype(BF16)

    def message(m, chunk):
        first, number, way = MESSAGES[m]
        return pltpu.make_async_remote_copy(
            src_ref=snd.at[chunk, pl.ds(first, number)],
            dst_ref=rcv.at[chunk, pl.ds(first, number)],
            send_sem=rs_send.at[chunk, m],
            recv_sem=rs_recv.at[chunk, m],
            device_id={"blk": peers[way]},
            device_id_type=pl.DeviceIdType.MESH,
        )

    def qg_copy(chunk):
        return pltpu.make_async_copy(
            qg.at[lax.rem(chunk, 2)],
            qg_hbm.at[0, :, pl.ds(pl.multiple_of(chunk * QW, QW), QW)],
            qg_sem.at[lax.rem(chunk, 2)],
        )

    def put(chunk, slot, value):
        snd[chunk, slot * HB : slot * HB + HB] = value.astype(BF16)

    def got(chunk, slot):
        return rcv[chunk, slot * HB : slot * HB + HB].astype(F32)

    def by_z(chunk, slot):
        return jnp.where(lax.broadcasted_iota(I32, (HB, CW), 0) < STAY, got(chunk, slot), 0.0)

    def by_x(chunk, slot):
        return jnp.where(lax.broadcasted_iota(I32, (HB, CW), 0) >= STAY, got(chunk, slot), 0.0)

    def kept(chunk, slot):
        return prod[lax.rem(chunk, 4), KEEP[slot]]

    def core_copy(k):
        return to(grad.at[k, 0], grad.at[k, 1], core_send.at[k], core_recv.at[k], dc=1)

    def dispatch(k):
        parts = []
        for chunk in range(PER):
            core_copy(k * PER + chunk).wait_recv()
        for part in range(2):
            for chip_core in range(2):
                first = part * BW
                while first < part * BW + BW:
                    width = min(BW, CW - first % CW)
                    parts.append(grad[k * PER + first // CW, chip_core, :, first % CW : first % CW + width])
                    first += width
        assert len(parts) == 4
        rows = jnp.concatenate(parts, axis=0)
        slots = jnp.dot(sel[...], rows, preferred_element_type=F32).astype(BF16)
        sent[k] = slots.reshape(PAIRS, 16, BW)
        landed[k, 0] = slots[0:16]
        for dz, dy, dx in AWAY:
            n = dz * 16 + dy * 4 + dx
            to(sent.at[k, n], landed.at[k, n], slot_send.at[k], slot_recv.at[k],
               dz=dz, dy=dy, dx=dx).start()

    def out_copy(chunk):
        return pltpu.make_async_copy(
            out.at[chunk],
            out_hbm.at[:, pl.ds(pl.multiple_of(chunk * 2 * BW, 2 * BW), 2 * BW)],
            out_sem.at[chunk],
        )

    def touch_down(k):
        whole(landed.at[k, pl.ds(1, PAIRS - 1)], slot_recv.at[k])
        total = jnp.dot(
            land[...], landed[k].reshape(16 * PAIRS, BW), preferred_element_type=F32
        )
        for part in range(2):
            out[k, :, part * BW : part * BW + BW] = total[part * HR : part * HR + HR]
        out_copy(k).start()

    def step(i, _):
        @pl.when(i < NC)
        def _():
            slab = lax.rem(i, 4)
            columns = pl.ds(pl.multiple_of(i * CW, CW), CW)
            def product(first, number):
                block = jnp.dot(
                    coef_t[first : first + number].reshape(number * HB, NQ), q[:, columns],
                    preferred_element_type=F32,
                ) * SCALE
                return block.reshape(number, HB, CW)

            block = product(10, 6)
            for k, slot in enumerate(Z2X + ZPX + ZMX[::-1]):
                put(i, k, block[slot - 10])
            for m in (0, 1, 2, 10, 11):
                message(m, i).start()
            block = product(0, 10)
            for slot, k in KEEP.items():
                prod[slab, k] = block[slot]
            put(i, 6, block[ZP])
            put(i, 7, block[ZM + 1])
            for m in (3, 4):
                message(m, i).start()

        @pl.when((i >= 1) & (i <= NC))
        def _():
            k = i - 1
            message(0, k).wait_recv()
            put(k, 9, kept(k, Z2) + got(k, 0))
            message(6, k).start()
            put(k, 8, kept(k, Z2 + 1) + got(k, 1))
            message(5, k).start()
            for m in (1, 2, 10, 11):
                message(m, k).wait_recv()
            put(k, 10, kept(k, XN) + got(k, 2) + by_z(k, 5))
            put(k, 11, kept(k, XN + 1) + by_z(k, 3) + got(k, 4))
            message(7, k).start()

        @pl.when((i >= 2) & (i <= NC + 1))
        def _():
            k = i - 2
            message(5, k).wait_recv()
            put(k, 12, kept(k, ZP + 1) + got(k, 8) + by_x(k, 3))
            message(8, k).start()
            message(6, k).wait_recv()
            put(k, 13, kept(k, ZM) + got(k, 9) + by_x(k, 5))
            message(9, k).start()

        @pl.when((i >= 3) & (i <= NC + 2))
        def _():
            k = i - 3
            for m in (3, 4, 7, 8, 9):
                message(m, k).wait_recv()
            low = kept(k, SELF) + got(k, 6) + got(k, 13) + got(k, 10)
            high = kept(k, SELF + 1) + got(k, 7) + got(k, 12) + got(k, 11)
            grad[k, 0, 0:HB] = low.astype(BF16)
            grad[k, 0, HB:CB] = high.astype(BF16)
            core_copy(k).start()

        @pl.when((i >= 3 + PER) & (lax.rem(i - 3, PER) == 0))
        def _():
            dispatch(lax.div(i - 3, PER) - 1)

        @pl.when(i == NC - 1)
        def _():
            for k in range(4):
                coef[pl.ds(k * 256, 256), :] = jnp.transpose(
                    coef_t[:, :, k * 256 : k * 256 + 256].reshape(16 * HB, 256)
                )

        @pl.when(i >= NC - 1)
        def _():
            query_part(i - (NC - 1))

        return 0

    def query_part(k):
        @pl.when(k >= 2)
        def _():
            qg_copy(k - 2).wait()

        for half in range(QW // 256):
            columns = pl.ds(pl.multiple_of(k * QW + half * 256, 256), 256)
            total = jnp.dot(
                coef[...], c[:, :, columns].reshape(16 * HB, 256), preferred_element_type=F32
            )
            qg[lax.rem(k, 2), :, half * 256 : half * 256 + 256] = (total * SCALE).astype(BF16)
        qg_copy(k).start()

    lax.fori_loop(0, NC + 4, step, 0)

    def land_part(k, _):
        touch_down(k)
        return 0

    lax.fori_loop(0, ND, land_part, 0)

    for copy in gather.values():
        copy.wait_send()

    for copy in tell_core + tell_x + tell_y + tell_z:
        copy.wait_send()

    def drain(i, _):
        for m in range(NM):
            message(m, i).wait_send()
        core_copy(i).wait_send()
        return 0

    lax.fori_loop(0, NC, drain, 0)
    for k in range(ND):
        whole(sent.at[k, pl.ds(1, PAIRS - 1)], slot_send.at[k])
        out_copy(k).wait()
    qg_copy(D // QW - 2).wait()
    qg_copy(D // QW - 1).wait()


def per_device(queries, candidates, loss_weight, positives, producers, rows):
    vmem, hbm = pl.BlockSpec(memory_space=pltpu.VMEM), pl.BlockSpec(memory_space=pl.ANY)
    shard_row = producers.reshape(1, CB)
    return pl.pallas_call(
        main_kernel,
        out_shape=(
            jax.ShapeDtypeStruct((1, NQ, D), BF16),
            jax.ShapeDtypeStruct((HR, D), F32),
        ),
        in_specs=[hbm, hbm, vmem, vmem, vmem, vmem],
        out_specs=(hbm, hbm),
        scratch_shapes=[
            pltpu.VMEM((NQ, D), BF16),
            pltpu.VMEM((16, HB, D), BF16),
            pltpu.VMEM((16, HB, NQ), F32),
            pltpu.VMEM((16, HB, NQ), BF16),
            pltpu.VMEM((NQ, 16 * HB), BF16),
            pltpu.VMEM((4, len(KEEP), HB, CW), F32),
            pltpu.VMEM((NC, 14 * HB, CW), BF16),
            pltpu.VMEM((NC, 14 * HB, CW), BF16),
            pltpu.VMEM((2, NQ, QW), BF16),
            pltpu.VMEM((16 * PAIRS, 4 * CB), BF16),
            pltpu.VMEM((8, NQ), F32),
            pltpu.VMEM((8, NQ), F32),
            pltpu.VMEM((4, 4, 4, 2, 2, CB), I32),
            pltpu.VMEM((2 * HR, 8 * SHARDS), BF16),
            pltpu.VMEM((ND, HR, 2 * BW), F32),
            pltpu.VMEM((NC, 2, CB, CW), BF16),
            pltpu.VMEM((ND, PAIRS, 16, BW), BF16),
            pltpu.VMEM((ND, PAIRS, 16, BW), BF16),
            pltpu.SemaphoreType.DMA,
            pltpu.SemaphoreType.DMA((2,)),
            pltpu.SemaphoreType.DMA((18,)),
            pltpu.SemaphoreType.DMA((18,)),
            pltpu.SemaphoreType.DMA((NC, NM)),
            pltpu.SemaphoreType.DMA((NC, NM)),
            pltpu.SemaphoreType.DMA((2,)),
            pltpu.SemaphoreType.DMA((ND,)),
            pltpu.SemaphoreType.DMA((10,)),
            pltpu.SemaphoreType.DMA((10,)),
            pltpu.SemaphoreType.DMA((NC,)),
            pltpu.SemaphoreType.DMA((NC,)),
            pltpu.SemaphoreType.DMA((ND,)),
            pltpu.SemaphoreType.DMA((ND,)),
        ],
        compiler_params=pltpu.CompilerParams(
            collective_id=0, has_side_effects=True, vmem_limit_bytes=62 * 2**20
        ),
        cost_estimate=pl.CostEstimate(
            flops=6 * NQ * NQ * D, bytes_accessed=20 * 2**20, transcendentals=NQ * NQ
        ),
        name="listwise_backward",
    )(queries, candidates, loss_weight, positives, shard_row, rows)


def solution(mesh):
    return jax.shard_map(
        per_device,
        mesh=mesh,
        in_specs=(
            P("dp", "blk", None),
            P("dp", "blk", None),
            P("dp", "blk"),
            P("dp", "blk"),
            P("dp", "blk", None),
            P("dp", "blk"),
        ),
        out_specs=(P("dp", "blk", None), P(("blk", "dp"), None)),
        check_vma=False,
    )
```
